1024 devices in a mesh: fsdp: 128 (over y, z, core), own: 8 (over x).
Axes of the slice: x: 8, y: 8, z: 8, core: 2. Of those that a mesh axis runs over, the one named last changes fastest.
Arguments:
- gradient: bfloat16 [128, 256, 256], P(None, 'fsdp'), may hold values from -6 to 6
- refresh: int32 [128, 2], P('fsdp'), may hold values 0 or 1
- left_stat: float32 [128, 256, 256], P('fsdp'), as said below
- right_stat: float32 [128, 256, 256], P('fsdp'), as said below
- left_root: bfloat16 [128, 256, 256], P('fsdp'), as said below
- right_root: bfloat16 [128, 256, 256], P('fsdp'), as said below
Outputs:
- grafted: bfloat16 [128, 256, 256], P(None, 'fsdp')
- new_left: float32 [128, 256, 256], P('fsdp')
- new_right: float32 [128, 256, 256], P('fsdp')
- new_left_root: bfloat16 [128, 256, 256], P('fsdp')
- new_right_root: bfloat16 [128, 256, 256], P('fsdp')
The draws below stay inside these ranges and needn't reach their ends.
Inputs may be any that keep to these rules, and one draw needn't show every extreme that they name: `left_stat`: each block is symmetric positive definite. `right_stat`: each block is symmetric positive definite. `left_root`: each block is symmetric. `right_root`: each block is symmetric.
All inputs are finite; a program needn't handle non-finite values. No bound on the sum of `refresh` on one device may be relied on, other than what follows from the above.
Results may differ from the reference program's by a relative error of at most 0.0053.
Values may be sent and summed in bfloat16 or wider, within the bound.
A program may use at most 32 MiB of HBM per device.

```python
import math
import jax
import jax.numpy as jnp
from jax import lax

B = 256
ITERS = 5
NBLK = 128


def symmetric_blocks(key, lower_end, upper_end, off_ratio):
    diag_key, noise_key = jax.random.split(key)
    diagonal_values = jnp.exp(jax.random.uniform(diag_key, (NBLK, B), jnp.float32, math.log(lower_end), math.log(upper_end)))
    noise_values = jax.random.uniform(noise_key, (NBLK, B, B), jnp.float32, -1.0, 1.0)
    symmetric = 0.5 * (noise_values + jnp.swapaxes(noise_values, 1, 2)) * (off_ratio * lower_end / math.sqrt(B))
    identity = jnp.eye(B, dtype=jnp.float32)
    return symmetric * (1.0 - identity) + identity * diagonal_values[:, :, None]


def draw_left_stat(key, part):
    key = jax.random.fold_in(key, 11)
    return symmetric_blocks(key, 64.0, 640.0, 0.6)


def draw_right_stat(key, part):
    key = jax.random.fold_in(key, 23)
    return symmetric_blocks(key, 64.0, 640.0, 0.6)


def draw_left_root(key, part):
    key = jax.random.fold_in(key, 37)
    return symmetric_blocks(key, 0.05, 0.5, 1.0).astype(jnp.bfloat16)


def draw_right_root(key, part):
    key = jax.random.fold_in(key, 41)
    return symmetric_blocks(key, 0.05, 0.5, 1.0).astype(jnp.bfloat16)


def with_ends(drawn, rng, smallest, high):
    index_at = [jax.random.randint(jax.random.fold_in(rng, axis), (), 0, length) for axis, length in enumerate(drawn.shape)]
    longest = drawn.shape.index(max(drawn.shape))
    neighbour = index_at[:longest] + [(index_at[longest] + 1) % drawn.shape[longest]] + index_at[longest + 1:]
    return drawn.at[tuple(index_at)].set(smallest).at[tuple(neighbour)].set(high)


def levels(stream_key, shape, cuts, low, largest):
    level, own = 1.0, jax.random.fold_in(stream_key, 6)
    for position, shards_of in cuts:
        steps = jnp.exp(jax.random.uniform(jax.random.fold_in(own, position), (shards_of,), jnp.float32, low / len(cuts), largest / len(cuts)))
        level = level * jnp.repeat(steps, shape[position] // shards_of).reshape([-1 if axis == position else 1 for axis in range(len(shape))])
    return level


def centred(rng, dims, spread, most, shards=(), held_as=jnp.bfloat16):
    level = levels(rng, dims, shards, -0.22, 0.18) if shards else 1.0
    values = jax.random.normal(rng, dims, jnp.float32) * spread * level
    return jnp.minimum(jnp.maximum(values, -most), most).astype(held_as)


def setup_inputs(seed: int = 0) -> dict:
    key_of = jax.random.split(jax.random.key(seed), 7)
    gradient = centred(key_of[0], (NBLK, B, B), 1.0, 6.0, ((1, 128),))
    refresh = with_ends((jax.random.randint(key_of[1], (NBLK, 2), 0, 8) < 1).astype(jnp.int32), jax.random.fold_in(key_of[1], 1), 0, 1)
    left_stat = draw_left_stat(jax.random.fold_in(key_of[6], 71), 0)
    right_stat = draw_right_stat(jax.random.fold_in(key_of[6], 71), 0)
    left_root = draw_left_root(jax.random.fold_in(key_of[6], 71), 0)
    right_root = draw_right_root(jax.random.fold_in(key_of[6], 71), 0)
    return dict(gradient=gradient, refresh=refresh, left_stat=left_stat, right_stat=right_stat, left_root=left_root, right_root=right_root)


decay_rate = 0.8
epsilon = 1e-06

def inverse_fourth_root(stat):
    identity = jnp.eye(stat.shape[0], dtype=jnp.float32)
    frobenius = jnp.sqrt(jnp.sum(stat * stat))
    matrix = stat / frobenius
    root_matrix = identity * frobenius ** (-0.25)
    for sweep in range(ITERS):
        factor = (5.0 * identity - matrix) * 0.25
        root_matrix = jnp.dot(root_matrix, factor, precision=lax.Precision.HIGHEST)
        square = jnp.dot(factor, factor, precision=lax.Precision.HIGHEST)
        fourth = jnp.dot(square, square, precision=lax.Precision.HIGHEST)
        matrix = jnp.dot(fourth, matrix, precision=lax.Precision.HIGHEST)
    return root_matrix

def per_block(operands):
    whole_block, flags, left_old, right_old, left_prev, right_prev = operands
    left_gram = lax.dot_general(whole_block, whole_block, (((1,), (1,)), ((), ())), preferred_element_type=jnp.float32)
    right_gram = lax.dot_general(whole_block, whole_block, (((0,), (0,)), ((), ())), preferred_element_type=jnp.float32)
    new_left = decay_rate * left_old + (1.0 - decay_rate) * left_gram
    new_right = decay_rate * right_old + (1.0 - decay_rate) * right_gram
    left_new = lax.cond(flags[0] == 1, lambda: inverse_fourth_root(new_left).astype(jnp.bfloat16), lambda: left_prev)
    right_new = lax.cond(flags[1] == 1, lambda: inverse_fourth_root(new_right).astype(jnp.bfloat16), lambda: right_prev)
    half_product = jnp.dot(left_new, whole_block, preferred_element_type=jnp.float32).astype(jnp.bfloat16)
    preconditioned = jnp.dot(half_product, right_new, preferred_element_type=jnp.float32)
    wide_block = whole_block.astype(jnp.float32)
    grad_norm = jnp.sqrt(jnp.sum(wide_block * wide_block))
    grafted = (preconditioned * (grad_norm / jnp.sqrt(jnp.sum(preconditioned * preconditioned) + epsilon))).astype(jnp.bfloat16)
    return (grafted, new_left, new_right, left_new, right_new)

def reference(gradient, refresh, left_stat, right_stat, left_root, right_root):
    results = lax.map(per_block, (gradient, refresh, left_stat, right_stat, left_root, right_root))
    return (results[0], results[1], results[2], results[3], results[4])
```

```python
import jax
import jax.numpy as jnp
from jax import lax
from jax.experimental import pallas as pl
from jax.experimental.pallas import tpu as pltpu
from jax.sharding import PartitionSpec as P

ITERS = 5
B = 256
Y, Z, C = 8, 8, 2

decay_rate = 0.8
epsilon = 1e-06

f32, bf16 = jnp.float32, jnp.bfloat16
MESH = pl.DeviceIdType.MESH


def dot(a, b, dims=((1,), (0,))):
    return lax.dot_general(a, b, (dims, ((), ())), preferred_element_type=f32)


def split(a):
    high = a.astype(bf16)
    return high, (a - high.astype(f32)).astype(bf16)


def product(a, b):
    return dot(a[0], b[0]) + (dot(a[0], b[1]) + dot(a[1], b[0]))


def inverse_fourth_roots(stats):
    n = range(len(stats))
    rows = lax.broadcasted_iota(jnp.int32, (B, B), 0)
    on_diagonal = rows == lax.broadcasted_iota(jnp.int32, (B, B), 1)
    frobenius = [jnp.sqrt(jnp.sum(s * s, keepdims=True)) for s in stats]
    matrix = [stats[i] / frobenius[i] for i in n]
    root = None
    for sweep in range(ITERS):
        parts = [split(m) for m in matrix]
        if root is None:
            root = [jnp.where(on_diagonal, 1.25, 0.0) - 0.25 * m for m in matrix]
        else:
            root = [1.25 * root[i] - 0.25 * product(split(root[i]), parts[i]) for i in n]
        if sweep < ITERS - 1:
            square = [product(parts[i], parts[i]) for i in n]
            r = [(square[i] - 10.0 * matrix[i]) * 0.0625 for i in n]
            rp = [split(x) for x in r]
            r4 = [3.125 * r[i] + product(rp[i], rp[i]) for i in n]
            matrix = [2.44140625 * matrix[i] + product(split(r4[i]), parts[i]) for i in n]
    scale = [jnp.exp(-0.25 * jnp.log(c)) for c in frobenius]
    return [root[i] * scale[i] for i in n]


def kernel(
    refresh_ref, g_ref, ls_ref, rs_ref, lr_ref, rr_ref,
    out_ref, nl_ref, nr_ref, nlr_ref, nrr_ref,
    relay, block, back, relay_back, ls, rs, lr, rr, nl, nr, nlr, nrr,
    load_sem, store_sem, send1, recv1, send2, recv2, send3, recv3, send4, recv4,
):
    me = lax.axis_index("fsdp")
    own = lax.axis_index("own")
    y, z, c = me // (Z * C), (me // C) % Z, me % C

    def at(py, pz, pc):
        return ((py * Z + pz) * C + pc, own)

    loads = [
        pltpu.make_async_copy(src, dst, load_sem.at[i])
        for i, (src, dst) in enumerate(((ls_ref, ls), (rs_ref, rs), (lr_ref, lr), (rr_ref, rr)))
    ]
    for copy in loads:
        copy.start()

    barrier = pltpu.get_barrier_semaphore()
    partners = 0
    for i in range(Y):
        for pc in range(C):
            if i:
                pl.semaphore_signal(barrier, inc=1, device_id=at((y + i) % Y, z, pc), device_id_type=MESH)
                pl.semaphore_signal(barrier, inc=1, device_id=at(y, (z + i) % Z, pc), device_id_type=MESH)
                partners += 2
    pl.semaphore_signal(barrier, inc=1, device_id=at(y, z, 1 - c), device_id_type=MESH)
    partners += 1
    pl.semaphore_wait(barrier, partners)

    def remote(src, dst, send, recv, to):
        return pltpu.make_async_remote_copy(
            src_ref=src, dst_ref=dst, send_sem=send, recv_sem=recv, device_id=to, device_id_type=MESH
        )

    def drained(ref, sem):
        pltpu.make_async_copy(ref, ref, sem).wait()

    for i in range(1, Z):
        pz = (z + i) % Z
        remote(g_ref.at[:, pz, 0], relay.at[:, z, c], send1, recv1, at(y, pz, 0)).start()
        py = (y + i) % Y
        remote(g_ref.at[py, :, 1], relay.at[:, y, c], send1, recv1, at(py, z, 1)).start()

    @pl.when(c == 0)
    def _():
        remote(g_ref.at[y, :, 1], relay.at[:, y, c], send1, recv1, at(y, z, 1)).start()
        pltpu.make_async_copy(g_ref.at[:, z, 0], relay.at[:, z, c], recv1).start()

    @pl.when(c == 1)
    def _():
        remote(g_ref.at[:, z, 0], relay.at[:, z, c], send1, recv1, at(y, z, 0)).start()
        pltpu.make_async_copy(g_ref.at[y, :, 1], relay.at[:, y, c], recv1).start()

    drained(relay, recv1)

    @pl.when(c == 0)
    def _():
        for i in range(1, Y):
            py = (y + i) % Y
            remote(relay.at[py], block.at[y], send2, recv2, at(py, z, 0)).start()
        pltpu.make_async_copy(relay.at[y], block.at[y], recv2).start()

    @pl.when(c == 1)
    def _():
        for i in range(1, Z):
            pz = (z + i) % Z
            remote(relay.at[pz], block.at[:, z], send2, recv2, at(y, pz, 1)).start()
        pltpu.make_async_copy(relay.at[z], block.at[:, z], recv2).start()

    drained(relay.at[:, 0:7], send1)
    drained(relay.at[:, 7, 0], send1)
    for copy in loads:
        copy.wait()
    drained(block, recv2)
    drained(block.at[0:7], send2)

    g = block[...].reshape(B, B)
    new_left = decay_rate * ls[...] + (1.0 - decay_rate) * dot(g, g, ((1,), (1,)))
    new_right = decay_rate * rs[...] + (1.0 - decay_rate) * dot(g, g, ((0,), (0,)))
    nl[...] = new_left
    nr[...] = new_right
    stores = [
        pltpu.make_async_copy(src, dst, store_sem.at[i])
        for i, (src, dst) in enumerate(((nl, nl_ref), (nr, nr_ref), (nlr, nlr_ref), (nrr, nrr_ref)))
    ]
    stores[0].start()
    stores[1].start()
    left_fresh, right_fresh = inverse_fourth_roots([new_left, new_right])
    left = jnp.where(refresh_ref[0, 0] == 1, left_fresh.astype(bf16), lr[...])
    right = jnp.where(refresh_ref[0, 1] == 1, right_fresh.astype(bf16), rr[...])
    nlr[...] = left
    nrr[...] = right
    stores[2].start()
    stores[3].start()
    preconditioned = dot(dot(left, g).astype(bf16), right)
    wide = g.astype(f32)
    grad_norm = jnp.sqrt(jnp.sum(wide * wide, keepdims=True))
    norm = jnp.sqrt(jnp.sum(preconditioned * preconditioned, keepdims=True) + epsilon)
    grafted = (preconditioned * (grad_norm / norm)).astype(bf16)
    back[...] = grafted.reshape(Y, Z, C, 2, B)

    @pl.when(c == 0)
    def _():
        for i in range(1, Y):
            py = (y + i) % Y
            remote(back.at[py], relay_back.at[y], send3, recv3, at(py, z, 0)).start()
        pltpu.make_async_copy(back.at[y], relay_back.at[y], recv3).start()

    @pl.when(c == 1)
    def _():
        for i in range(1, Z):
            pz = (z + i) % Z
            remote(back.at[:, pz], relay_back.at[z], send3, recv3, at(y, pz, 1)).start()
        pltpu.make_async_copy(back.at[:, z], relay_back.at[z], recv3).start()

    drained(relay_back, recv3)

    @pl.when(c == 0)
    def _():
        for i in range(1, Z):
            for pc in range(C):
                pz = (z + i) % Z
                remote(relay_back.at[:, pz, pc], out_ref.at[:, z, 0], send4, recv4, at(y, pz, pc)).start()
        remote(relay_back.at[:, z, 1], out_ref.at[:, z, 0], send4, recv4, at(y, z, 1)).start()
        pltpu.make_async_copy(relay_back.at[:, z, 0], out_ref.at[:, z, 0], recv4).start()

    @pl.when(c == 1)
    def _():
        for i in range(1, Y):
            for pc in range(C):
                py = (y + i) % Y
                remote(relay_back.at[:, py, pc], out_ref.at[y, :, 1], send4, recv4, at(py, z, pc)).start()
        remote(relay_back.at[:, y, 0], out_ref.at[y, :, 1], send4, recv4, at(y, z, 0)).start()
        pltpu.make_async_copy(relay_back.at[:, y, 1], out_ref.at[y, :, 1], recv4).start()

    drained(relay_back.at[0:7], send3)
    for copy in stores:
        copy.wait()
    drained(relay_back.at[:, 0:7], send4)
    drained(relay_back.at[:, 7, 0], send4)
    drained(out_ref, recv4)


def shards(gradient, refresh, left_stat, right_stat, left_root, right_root):
    anywhere = pl.BlockSpec(memory_space=pl.ANY)
    square = lambda dtype: jax.ShapeDtypeStruct((B, B), dtype)
    rows = (Y, Z, C, 2, B)
    dma = pltpu.SemaphoreType.DMA
    grafted, new_left, new_right, new_left_root, new_right_root = pl.pallas_call(
        kernel,
        out_shape=(jax.ShapeDtypeStruct(rows, bf16), square(f32), square(f32), square(bf16), square(bf16)),
        in_specs=[pl.BlockSpec(memory_space=pltpu.SMEM)] + [anywhere] * 5,
        out_specs=(anywhere,) * 5,
        scratch_shapes=[pltpu.VMEM(rows, bf16)] * 4
        + [pltpu.VMEM((B, B), t) for t in (f32, f32, bf16, bf16, f32, f32, bf16, bf16)]
        + [dma((4,)), dma((4,))]
        + [dma] * 8,
        compiler_params=pltpu.CompilerParams(
            collective_id=0, has_side_effects=True, vmem_limit_bytes=32 * 1024 * 1024
        ),
    )(
        refresh, gradient.reshape(rows), left_stat[0], right_stat[0], left_root[0], right_root[0]
    )
    return (
        grafted.reshape(Y * Z * C, 2, B), new_left[None], new_right[None], new_left_root[None], new_right_root[None]
    )


def solution(mesh):
    rows, blocks = P(None, "fsdp", None), P("fsdp", None, None)
    return jax.shard_map(
        shards,
        mesh=mesh,
        in_specs=(rows, P("fsdp", None), blocks, blocks, blocks, blocks),
        out_specs=(rows, blocks, blocks, blocks, blocks),
        check_vma=False,
    )
```

```python
import jax
import jax.numpy as jnp
from jax import lax
from jax.experimental import pallas as pl
from jax.experimental.pallas import tpu as pltpu
from jax.sharding import PartitionSpec as P

ITERS = 5
B = 256
X, Y, Z, C = 8, 8, 8, 2
GROUP = Z * C * 2

decay_rate = 0.8
epsilon = 1e-06

f32, bf16 = jnp.float32, jnp.bfloat16
MESH = pl.DeviceIdType.MESH


def dot(a, b, dims=((1,), (0,))):
    return lax.dot_general(a, b, (dims, ((), ())), preferred_element_type=f32)


def split(a):
    high = a.astype(bf16)
    return high, (a - high.astype(f32)).astype(bf16)


def product(a, b):
    return dot(a[0], b[0]) + (dot(a[0], b[1]) + dot(a[1], b[0]))


def inverse_fourth_roots(stats):
    n = range(len(stats))
    rows = lax.broadcasted_iota(jnp.int32, (B, B), 0)
    on_diagonal = rows == lax.broadcasted_iota(jnp.int32, (B, B), 1)
    frobenius = [jnp.sqrt(jnp.sum(s * s, keepdims=True)) for s in stats]
    matrix = [stats[i] / frobenius[i] for i in n]
    root = None
    for sweep in range(ITERS):
        parts = [split(m) for m in matrix]
        if root is None:
            root = [jnp.where(on_diagonal, 1.25, 0.0) - 0.25 * m for m in matrix]
        else:
            root = [1.25 * root[i] - 0.25 * product(split(root[i]), parts[i]) for i in n]
        if sweep < ITERS - 1:
            square = [product(parts[i], parts[i]) for i in n]
            r = [(square[i] - 10.0 * matrix[i]) * 0.0625 for i in n]
            rp = [split(x) for x in r]
            r4 = [3.125 * r[i] + product(rp[i], rp[i]) for i in n]
            matrix = [2.44140625 * matrix[i] + product(split(r4[i]), parts[i]) for i in n]
    scale = [jnp.exp(-0.25 * jnp.log(c)) for c in frobenius]
    return [root[i] * scale[i] for i in n]


def kernel(
    refresh_ref, g_ref, ls_ref, rs_ref, lr_ref, rr_ref,
    out_ref, nl_ref, nr_ref, nlr_ref, nrr_ref,
    refresh, relay, relay_rows, block, pre, back, relay_back, ls, rs, lr, rr, nl, nr, nlr, nrr,
    load_sem, store_sem, send1, recv1, send2, recv2, send3, recv3, send4, recv4,
):
    me, x = lax.axis_index("fsdp"), lax.axis_index("own")
    y, z, c = me // (Z * C), (me // C) % Z, me % C
    y_to = (x + Y - y) % Y

    def at(px, py, pz, pc):
        return ((py * Z + pz) * C + pc, px)

    loads = [
        pltpu.make_async_copy(src, dst, load_sem.at[i])
        for i, (src, dst) in enumerate(
            ((refresh_ref, refresh), (ls_ref, ls), (rs_ref, rs), (lr_ref, lr), (rr_ref, rr))
        )
    ]

    peers = [((z + i) % Z, (c + j) % C) for i in range(Z) for j in range(C)][1:]
    barrier = pltpu.get_barrier_semaphore()

    def greet(device):
        pl.semaphore_signal(barrier, inc=1, device_id=device, device_id_type=MESH)

    for pz, pc in peers:
        greet(at(x, y, pz, pc))
    for i in range(1, X):
        px = (x + i) % X
        greet(at(px, (px + Y - y) % Y, z, c))

    @pl.when(y_to != y)
    def _():
        greet(at(x, y_to, z, c))

    for copy in loads:
        copy.start()
    pl.semaphore_wait(barrier, len(peers) + X - 1 + (y_to != y).astype(jnp.int32))

    def remote(src, dst, send, recv, to):
        pltpu.make_async_remote_copy(
            src_ref=src, dst_ref=dst, send_sem=send, recv_sem=recv, device_id=to, device_id_type=MESH
        ).start()

    def drained(ref, sem):
        pltpu.make_async_copy(ref, ref, sem).wait()

    def among_peers(src, dst, send, recv):
        for pz, pc in peers:
            remote(src.at[pz, pc], dst.at[z, c], send, recv, at(x, y, pz, pc))
        pltpu.make_async_copy(src.at[z, c], dst.at[z, c], recv).start()

    def to_replicas(src, dst, send, recv):
        for i in range(1, X):
            remote(src, dst, send, recv, at((x + i) % X, y_to, z, c))

        @pl.when(y_to != y)
        def _():
            remote(src, dst, send, recv, at(x, y_to, z, c))

        @pl.when(y_to == y)
        def _():
            pltpu.make_async_copy(src, dst, recv).start()

    def sent_to_peers(ref, sem):
        drained(ref.at[1:Z], sem)
        drained(ref.at[0, 0], sem)

    def sent_to_replicas(ref, sem):
        for i in range(1, X):
            drained(ref, sem)

        @pl.when(y_to != y)
        def _():
            drained(ref, sem)

    among_peers(g_ref.at[y_to], relay, send1, recv1)
    drained(relay, recv1)
    relay_rows[...] = relay[...].reshape(GROUP, B)
    to_replicas(relay_rows, block.at[pl.ds(pl.multiple_of(y * GROUP, GROUP), GROUP)], send2, recv2)
    for copy in loads:
        copy.wait()
    drained(block, recv2)

    g = block[...]
    new_left = decay_rate * ls[...] + (1.0 - decay_rate) * dot(g, g, ((1,), (1,)))
    new_right = decay_rate * rs[...] + (1.0 - decay_rate) * dot(g, g, ((0,), (0,)))
    nl[...] = new_left
    nr[...] = new_right
    stores = [
        pltpu.make_async_copy(src, dst, store_sem.at[i])
        for i, (src, dst) in enumerate(((nl, nl_ref), (nr, nr_ref), (nlr, nlr_ref), (nrr, nrr_ref)))
    ]
    stores[0].start()
    stores[1].start()
    left_fresh, right_fresh = inverse_fourth_roots([new_left, new_right])
    left = jnp.where(refresh[0, 0] == 1, left_fresh.astype(bf16), lr[...])
    right = jnp.where(refresh[0, 1] == 1, right_fresh.astype(bf16), rr[...])
    nlr[...] = left
    nrr[...] = right
    stores[2].start()
    stores[3].start()
    preconditioned = dot(dot(left, g).astype(bf16), right)
    pre[...] = preconditioned
    wide = g.astype(f32)
    grad_norm = jnp.sqrt(jnp.sum(wide * wide, keepdims=True))
    norm = jnp.sqrt(jnp.sum(preconditioned * preconditioned, keepdims=True) + epsilon)
    rows = pre[pl.ds(pl.multiple_of(y_to * GROUP, GROUP), GROUP), :]
    back[...] = (rows * (grad_norm / norm)).astype(bf16).reshape(Z, C, 2, B)

    among_peers(back, relay_back, send3, recv3)
    drained(relay_back, recv3)
    to_replicas(relay_back, out_ref.at[y], send4, recv4)

    sent_to_peers(relay, send1)
    sent_to_replicas(relay_rows, send2)
    sent_to_peers(back, send3)
    for copy in stores:
        copy.wait()
    sent_to_replicas(relay_back, send4)
    drained(out_ref, recv4)


def write_out(*refs):
    n = len(refs) // 2
    sem = refs[-1]
    copies = [pltpu.make_async_copy(refs[i], refs[n + i], sem.at[i]) for i in range(n)]
    for copy in copies:
        copy.start()
    for copy in copies:
        copy.wait()


def shards(gradient, refresh, left_stat, right_stat, left_root, right_root):
    anywhere = pl.BlockSpec(memory_space=pl.ANY)
    square = lambda dtype: jax.ShapeDtypeStruct((B, B), dtype)
    outs = (jax.ShapeDtypeStruct((Y, Z, C, 2, B), bf16), square(f32), square(f32), square(bf16), square(bf16))
    dma = pltpu.SemaphoreType.DMA
    results = pl.pallas_call(
        kernel,
        out_shape=outs,
        in_specs=[anywhere] * 6,
        out_specs=(anywhere,) * 5,
        scratch_shapes=[
            pltpu.SMEM((1, 2), jnp.int32),
            pltpu.VMEM((Z, C, 2, B), bf16),
            pltpu.VMEM((GROUP, B), bf16),
            pltpu.VMEM((B, B), bf16),
            pltpu.VMEM((B, B), f32),
            pltpu.VMEM((Z, C, 2, B), bf16),
            pltpu.VMEM((Z, C, 2, B), bf16),
        ]
        + [pltpu.VMEM((B, B), t) for t in (f32, f32, bf16, bf16, f32, f32, bf16, bf16)]
        + [dma((5,)), dma((4,))]
        + [dma] * 8,
        compiler_params=pltpu.CompilerParams(collective_id=0, has_side_effects=True),
    )(
        refresh, gradient.reshape(Y, Z, C, 2, B), left_stat[0], right_stat[0], left_root[0], right_root[0]
    )
    grafted, new_left, new_right, new_left_root, new_right_root = pl.pallas_call(
        write_out,
        out_shape=outs,
        in_specs=[anywhere] * 5,
        out_specs=(anywhere,) * 5,
        scratch_shapes=[dma((5,))],
    )(*results)
    return (
        grafted.reshape(Y * Z * C, 2, B), new_left[None], new_right[None], new_left_root[None], new_right_root[None]
    )


def solution(mesh):
    rows, blocks = P(None, "fsdp", None), P("fsdp", None, None)
    return jax.shard_map(
        shards,
        mesh=mesh,
        in_specs=(rows, P("fsdp", None), blocks, blocks, blocks, blocks),
        out_specs=(rows, blocks, blocks, blocks, blocks),
        check_vma=False,
    )
```

```python
import jax
import jax.numpy as jnp
from jax import lax
from jax.experimental import pallas as pl
from jax.experimental.pallas import tpu as pltpu
from jax.sharding import PartitionSpec as P

ITERS = 5
B = 256
Y, Z, C = 8, 8, 2

decay_rate = 0.8
epsilon = 1e-06

f32, bf16 = jnp.float32, jnp.bfloat16
MESH = pl.DeviceIdType.MESH


def dot(a, b, dims=((1,), (0,))):
    return lax.dot_general(a, b, (dims, ((), ())), preferred_element_type=f32)


def split(a):
    high = a.astype(bf16)
    return high, (a - high.astype(f32)).astype(bf16)


def product(a, b):
    return dot(a[0], b[0]) + (dot(a[0], b[1]) + dot(a[1], b[0]))


def inverse_fourth_roots(stats):
    n = range(len(stats))
    rows = lax.broadcasted_iota(jnp.int32, (B, B), 0)
    on_diagonal = rows == lax.broadcasted_iota(jnp.int32, (B, B), 1)
    frobenius = [jnp.sqrt(jnp.sum(s * s, keepdims=True)) for s in stats]
    matrix = [stats[i] / frobenius[i] for i in n]
    root = None
    for sweep in range(ITERS):
        parts = [split(m) for m in matrix]
        if root is None:
            root = [jnp.where(on_diagonal, 1.25, 0.0) - 0.25 * m for m in matrix]
        else:
            root = [1.25 * root[i] - 0.25 * product(split(root[i]), parts[i]) for i in n]
        if sweep < ITERS - 1:
            square = [product(parts[i], parts[i]) for i in n]
            r = [(square[i] - 10.0 * matrix[i]) * 0.0625 for i in n]
            rp = [split(x) for x in r]
            r4 = [3.125 * r[i] + product(rp[i], rp[i]) for i in n]
            matrix = [2.44140625 * matrix[i] + product(split(r4[i]), parts[i]) for i in n]
    scale = [jnp.exp(-0.25 * jnp.log(c)) for c in frobenius]
    return [root[i] * scale[i] for i in n]


def kernel(
    refresh_ref, g_ref, ls_ref, rs_ref, lr_ref, rr_ref,
    out_ref, nl_ref, nr_ref, nlr_ref, nrr_ref,
    refresh, relay, block, back, relay_back, sorted_back, landed, ls, rs, lr, rr, nl, nr, nlr, nrr,
    load_sem, store_sem, send1, recv1, send2, recv2, send3, recv3, send4, recv4, here,
):
    me, own = lax.axis_index("fsdp"), lax.axis_index("own")
    y, z, c = me // (Z * C), (me // C) % Z, me % C

    def at(py, pz, pc):
        return ((py * Z + pz) * C + pc, own)

    loads = [
        pltpu.make_async_copy(src, dst, load_sem.at[i])
        for i, (src, dst) in enumerate(
            ((refresh_ref, refresh), (ls_ref, ls), (rs_ref, rs), (lr_ref, lr), (rr_ref, rr))
        )
    ]

    row = [((y + i) % Y, (c + j) % C) for i in range(Y) for j in range(C)][1:]
    barrier = pltpu.get_barrier_semaphore()
    for py, pc in row:
        pl.semaphore_signal(barrier, inc=1, device_id=at(py, z, pc), device_id_type=MESH)
    for pz in range(1, Z):

        @pl.when(pz > z)
        def _():
            pl.semaphore_signal(barrier, inc=1, device_id=at(y, pz, c), device_id_type=MESH)

    for copy in loads:
        copy.start()
    pl.semaphore_wait(barrier, len(row) + z)
    for pz in range(Z - 1):

        @pl.when(pz < z)
        def _():
            pl.semaphore_signal(here.at[z], inc=1, device_id=at(y, pz, c), device_id_type=MESH)

    def remote(src, dst, send, recv, to):
        pltpu.make_async_remote_copy(
            src_ref=src, dst_ref=dst, send_sem=send, recv_sem=recv, device_id=to, device_id_type=MESH
        ).start()

    def drained(ref, sem):
        pltpu.make_async_copy(ref, ref, sem).wait()

    for py, pc in row[::-1]:
        remote(g_ref.at[py, :, pc], relay.at[:, y, c], send1, recv1, at(py, z, pc))
    pltpu.make_async_copy(g_ref.at[y, :, c], relay.at[:, y, c], recv1).start()
    drained(relay, recv1)

    for pz in range(Z):

        @pl.when(pz > z)
        def _():
            pl.semaphore_wait(here.at[pz], 1)

        @pl.when(pz != z)
        def _():
            remote(relay.at[pz], block.at[:, z], send2, recv2, at(y, pz, c))

    pltpu.make_async_copy(relay.at[z], block.at[:, z], recv2).start()
    for copy in loads:
        copy.wait()
    drained(block, recv2)

    g = block[...].reshape(B, B)
    new_left = decay_rate * ls[...] + (1.0 - decay_rate) * dot(g, g, ((1,), (1,)))
    new_right = decay_rate * rs[...] + (1.0 - decay_rate) * dot(g, g, ((0,), (0,)))
    nl[...] = new_left
    nr[...] = new_right
    stores = [
        pltpu.make_async_copy(src, dst, store_sem.at[i])
        for i, (src, dst) in enumerate(((nl, nl_ref), (nr, nr_ref), (nlr, nlr_ref), (nrr, nrr_ref)))
    ]
    stores[0].start()
    stores[1].start()
    left_fresh, right_fresh = inverse_fourth_roots([new_left, new_right])
    left = jnp.where(refresh[0, 0] == 1, left_fresh.astype(bf16), lr[...])
    right = jnp.where(refresh[0, 1] == 1, right_fresh.astype(bf16), rr[...])
    nlr[...] = left
    nrr[...] = right
    stores[2].start()
    stores[3].start()
    preconditioned = dot(dot(left, g).astype(bf16), right)
    wide = g.astype(f32)
    grad_norm = jnp.sqrt(jnp.sum(wide * wide, keepdims=True))
    norm = jnp.sqrt(jnp.sum(preconditioned * preconditioned, keepdims=True) + epsilon)
    grafted = (preconditioned * (grad_norm / norm)).astype(bf16)
    back[...] = grafted.reshape(Y, Z, C, 2, B)

    for i in (4, 3, 5, 2, 6, 1, 7):
        py = (y + i) % Y
        remote(back.at[py], relay_back.at[y], send3, recv3, at(py, z, c))
    pltpu.make_async_copy(back.at[y], relay_back.at[y], recv3).start()
    drained(relay_back, recv3)

    for pz in range(Z):
        for pc in range(C):
            sorted_back[pz, pc] = relay_back[:, pz, pc]

            @pl.when((pz != z) | (pc != c))
            def _():
                remote(sorted_back.at[pz, pc], landed.at[z, c], send4, recv4, at(y, pz, pc))

    pltpu.make_async_copy(sorted_back.at[z, c], landed.at[z, c], recv4).start()

    drained(relay.at[1:], send1)
    drained(relay.at[0, 0:4], send1)
    drained(block.at[1:], send2)
    drained(relay_back.at[1:], send3)
    for copy in stores:
        copy.wait()
    drained(landed, recv4)
    out_ref[...] = landed[...]
    drained(landed.at[1:], send4)
    drained(landed.at[0, 0], send4)


def write_out(rows_ref, nl_in, nr_in, nlr_in, nrr_in, out_ref, nl_ref, nr_ref, nlr_ref, nrr_ref, sem):
    copies = [pltpu.make_async_copy(rows_ref.at[:, :, y], out_ref.at[y], sem.at[y]) for y in range(Y)]
    copies += [
        pltpu.make_async_copy(src, dst, sem.at[Y + i])
        for i, (src, dst) in enumerate(((nl_in, nl_ref), (nr_in, nr_ref), (nlr_in, nlr_ref), (nrr_in, nrr_ref)))
    ]
    for copy in copies:
        copy.start()
    for copy in copies:
        copy.wait()


def shards(gradient, refresh, left_stat, right_stat, left_root, right_root):
    anywhere = pl.BlockSpec(memory_space=pl.ANY)
    vmem = pl.BlockSpec(memory_space=pltpu.VMEM)
    square = lambda dtype: jax.ShapeDtypeStruct((B, B), dtype)
    squares = (square(f32), square(f32), square(bf16), square(bf16))
    rows = (Y, Z, C, 2, B)
    dma = pltpu.SemaphoreType.DMA
    operands = (
        refresh, gradient.reshape(rows), left_stat[0], right_stat[0], left_root[0], right_root[0]
    )
    results = pl.pallas_call(
        kernel,
        out_shape=(jax.ShapeDtypeStruct((Z, C, Y, 2, B), bf16),) + squares,
        in_specs=[anywhere] * 6,
        out_specs=(vmem,) + (anywhere,) * 4,
        scratch_shapes=[pltpu.SMEM((1, 2), jnp.int32)]
        + [pltpu.VMEM(r, bf16) for r in ((Z, Y, C, 2, B), rows, rows, rows, (Z, C, Y, 2, B), (Z, C, Y, 2, B))]
        + [pltpu.VMEM((B, B), t) for t in (f32, f32, bf16, bf16, f32, f32, bf16, bf16)]
        + [dma((5,)), dma((4,))]
        + [dma] * 8
        + [pltpu.SemaphoreType.REGULAR((Z,))],
        compiler_params=pltpu.CompilerParams(
            collective_id=0, has_side_effects=True, vmem_limit_bytes=32 * 1024 * 1024
        ),
    )(*[pltpu.with_memory_space_constraint(x, pltpu.HBM) for x in operands])
    grafted, new_left, new_right, new_left_root, new_right_root = pl.pallas_call(
        write_out,
        out_shape=(jax.ShapeDtypeStruct(rows, bf16),) + squares,
        in_specs=[vmem] * 5,
        out_specs=(anywhere,) * 5,
        scratch_shapes=[dma((Y + 4,))],
        compiler_params=pltpu.CompilerParams(vmem_limit_bytes=32 * 1024 * 1024),
    )(*results)
    return (
        grafted.reshape(Y * Z * C, 2, B), new_left[None], new_right[None], new_left_root[None], new_right_root[None]
    )


def solution(mesh):
    rows, blocks = P(None, "fsdp", None), P("fsdp", None, None)
    return jax.shard_map(
        shards,
        mesh=mesh,
        in_specs=(rows, P("fsdp", None), blocks, blocks, blocks, blocks),
        out_specs=(rows, blocks, blocks, blocks, blocks),
        check_vma=False,
    )
```

```python
import functools

import jax
import jax.numpy as jnp
from jax import lax
from jax.experimental import pallas as pl
from jax.experimental.pallas import tpu as pltpu
from jax.sharding import PartitionSpec as P

ITERS = 5
B = 256
Y, Z, C = 8, 8, 2

decay_rate = 0.8
epsilon = 1e-06

f32, bf16 = jnp.float32, jnp.bfloat16
MESH = pl.DeviceIdType.MESH


def dot(a, b, dims=((1,), (0,))):
    return lax.dot_general(a, b, (dims, ((), ())), preferred_element_type=f32)


def split(a):
    high = a.astype(bf16)
    return high, (a - high.astype(f32)).astype(bf16)


def product(a, b):
    return dot(a[0], b[0]) + (dot(a[0], b[1]) + dot(a[1], b[0]))


def inverse_fourth_roots(stats):
    n = range(len(stats))
    rows = lax.broadcasted_iota(jnp.int32, (B, B), 0)
    on_diagonal = rows == lax.broadcasted_iota(jnp.int32, (B, B), 1)
    frobenius = [jnp.sqrt(jnp.sum(s * s, keepdims=True)) for s in stats]
    matrix = [stats[i] / frobenius[i] for i in n]
    root = None
    for sweep in range(ITERS):
        parts = [split(m) for m in matrix]
        if root is None:
            root = [jnp.where(on_diagonal, 1.25, 0.0) - 0.25 * m for m in matrix]
        else:
            root = [1.25 * root[i] - 0.25 * product(split(root[i]), parts[i]) for i in n]
        if sweep < ITERS - 1:
            square = [product(parts[i], parts[i]) for i in n]
            r = [(square[i] - 10.0 * matrix[i]) * 0.0625 for i in n]
            rp = [split(x) for x in r]
            r4 = [3.125 * r[i] + product(rp[i], rp[i]) for i in n]
            matrix = [2.44140625 * matrix[i] + product(split(r4[i]), parts[i]) for i in n]
    scale = [jnp.exp(-0.25 * jnp.log(c)) for c in frobenius]
    return [root[i] * scale[i] for i in n]


def kernel(
    refresh_ref, g_ref, ls_ref, rs_ref, lr_ref, rr_ref,
    out_ref, nl_ref, nr_ref, nlr_ref, nrr_ref,
    refresh, both, relay, block, back, both_back, ls, rs, lr, rr, nl, nr, nlr, nrr,
    load_sem, store_sem, send_core, recv_core, send_row, send_down, send_up, recv_relay, recv_block,
    send_back, recv_back, send_out, recv_out, here_row, here_up,
):
    me, own = lax.axis_index("fsdp"), lax.axis_index("own")
    y, z, c = me // (Z * C), (me // C) % Z, me % C
    ORDER = (0, 1, 2, 3, 6, 7, 4, 5)
    rank = jnp.where(y < 4, y, (y + 2) % 4 + 4)

    def at(py, pz, pc=c):
        return ((py * Z + pz) * C + pc, own)

    def signal(sem, device):
        pl.semaphore_signal(sem, inc=1, device_id=device, device_id_type=MESH)

    def remote(src, dst, send, recv, to):
        pltpu.make_async_remote_copy(
            src_ref=src, dst_ref=dst, send_sem=send, recv_sem=recv, device_id=to, device_id_type=MESH
        ).start()

    def local(src, dst, sem):
        pltpu.make_async_copy(src, dst, sem).start()

    def drained(ref, sem):
        pltpu.make_async_copy(ref, ref, sem).wait()

    def repeat(low, high, body):
        def step(i, carry):
            body(i)
            return carry

        lax.fori_loop(low, high, step, 0)

    barrier = pltpu.get_barrier_semaphore()
    signal(barrier, at(y, z, 1 - c))
    for r in range(1, Y):

        @pl.when(r > rank)
        def _():
            signal(barrier, at(ORDER[r], z))

    @functools.partial(repeat, z + 1, Z)
    def _(pz):
        for py in range(Y):
            signal(barrier, at(py, pz))

    loads = [
        pltpu.make_async_copy(src, dst, load_sem.at[i])
        for i, (src, dst) in enumerate(
            ((refresh_ref, refresh), (ls_ref, ls), (rs_ref, rs), (lr_ref, lr), (rr_ref, rr))
        )
    ]
    for copy in loads:
        copy.start()
    pl.semaphore_wait(barrier, 1 + rank + Y * z)
    for r in range(Y - 1):

        @pl.when(r < rank)
        def _():
            signal(here_row.at[rank], at(ORDER[r], z))

    @functools.partial(repeat, 0, z)
    def _(pz):
        signal(here_up.at[z], at(y, pz))

    remote(g_ref.at[:, :, 1 - c], both.at[:, :, c], send_core, recv_core, at(y, z, 1 - c))
    local(g_ref.at[:, :, c], both.at[:, :, c], recv_core)
    drained(both, recv_core)

    def to_row(py):
        remote(both.at[py, z], block.at[y, z], send_row, recv_block, at(py, z))

        @functools.partial(repeat, z + 1, Z)
        def _(pz):
            remote(both.at[py, pz], relay.at[pz, y], send_row, recv_relay.at[pz], at(py, z))

    for r in range(Y - 1):

        @pl.when(r < rank)
        def _():
            to_row(ORDER[r])

    def to_lower(pz):
        for py in range(Y):
            remote(both.at[py, pz], block.at[y, z], send_down, recv_block, at(py, pz))

    @functools.partial(repeat, 0, z)
    def _(i):
        to_lower(lax.rem(i + z // 2, z))

    local(both.at[y, z], block.at[y, z], recv_block)

    @functools.partial(repeat, z + 1, Z)
    def _(pz):
        local(both.at[y, pz], relay.at[pz, y], recv_relay.at[pz])

    for r in range(1, Y):

        @pl.when(r > rank)
        def _():
            pl.semaphore_wait(here_row.at[r], 1)
            to_row(ORDER[r])

    @functools.partial(repeat, z + 1, Z)
    def _(pz):
        drained(relay.at[pz], recv_relay.at[pz])
        pl.semaphore_wait(here_up.at[pz], 1)
        remote(relay.at[pz], block.at[:, z], send_up, recv_block, at(y, pz))

    drained(both.at[:, :, 0], send_core)
    repeat(z, Z, lambda i: drained(relay.at[0, 1:], send_row))
    repeat(0, z, lambda i: drained(relay.at[0], send_down))
    repeat(z + 1, Z, lambda i: drained(relay.at[0], send_up))
    for copy in loads:
        copy.wait()
    drained(block, recv_block)

    g = block[...].reshape(B, B)
    new_left = decay_rate * ls[...] + (1.0 - decay_rate) * dot(g, g, ((1,), (1,)))
    new_right = decay_rate * rs[...] + (1.0 - decay_rate) * dot(g, g, ((0,), (0,)))
    nl[...] = new_left
    nr[...] = new_right
    stores = [
        pltpu.make_async_copy(src, dst, store_sem.at[i])
        for i, (src, dst) in enumerate(((nl, nl_ref), (nr, nr_ref), (nlr, nlr_ref), (nrr, nrr_ref)))
    ]
    stores[0].start()
    stores[1].start()
    left_fresh, right_fresh = inverse_fourth_roots([new_left, new_right])
    left = jnp.where(refresh[0, 0] == 1, left_fresh.astype(bf16), lr[...])
    right = jnp.where(refresh[0, 1] == 1, right_fresh.astype(bf16), rr[...])
    nlr[...] = left
    nrr[...] = right
    stores[2].start()
    stores[3].start()
    preconditioned = dot(dot(left, g).astype(bf16), right)
    wide = g.astype(f32)
    grad_norm = jnp.sqrt(jnp.sum(wide * wide, keepdims=True))
    norm = jnp.sqrt(jnp.sum(preconditioned * preconditioned, keepdims=True) + epsilon)
    grafted = (preconditioned * (grad_norm / norm)).astype(bf16)
    back[...] = grafted.reshape(Y, Z, C, 2, B)

    remote(back.at[:, :, 1 - c], both_back.at[:, :, c], send_back, recv_back, at(y, z, 1 - c))
    local(back.at[:, :, c], both_back.at[:, :, c], recv_back)
    drained(both_back, recv_back)

    @functools.partial(repeat, 0, Z)
    def _(pz):
        for i in (4, 3, 5, 2, 6, 1, 7):
            py = (y + i) % Y
            remote(both_back.at[py, pz], out_ref.at[y, z], send_out, recv_out, at(py, pz))

        @pl.when(pz != z)
        def _():
            remote(both_back.at[y, pz], out_ref.at[y, z], send_out, recv_out, at(y, pz))

    local(both_back.at[y, z], out_ref.at[y, z], recv_out)
    drained(both_back.at[:, :, 0], send_back)
    for copy in stores:
        copy.wait()
    drained(out_ref, recv_out)
    drained(both_back.at[1:], send_out)
    drained(both_back.at[0, 1:], send_out)


def write_out(*refs):
    n = len(refs) // 2
    copies = [pltpu.make_async_copy(refs[i], refs[n + i], refs[-1].at[i]) for i in range(n)]
    for copy in copies:
        copy.start()
    for copy in copies:
        copy.wait()


def shards(gradient, refresh, left_stat, right_stat, left_root, right_root):
    anywhere = pl.BlockSpec(memory_space=pl.ANY)
    square = lambda dtype: jax.ShapeDtypeStruct((B, B), dtype)
    rows = (Y, Z, C, 2, B)
    outs = (jax.ShapeDtypeStruct(rows, bf16), square(f32), square(f32), square(bf16), square(bf16))
    dma, regular = pltpu.SemaphoreType.DMA, pltpu.SemaphoreType.REGULAR
    operands = (
        refresh, gradient.reshape(rows), left_stat[0], right_stat[0], left_root[0], right_root[0]
    )
    results = pl.pallas_call(
        kernel,
        out_shape=outs,
        in_specs=[anywhere] * 6,
        out_specs=(anywhere,) * 5,
        scratch_shapes=[pltpu.SMEM((1, 2), jnp.int32)]
        + [pltpu.VMEM(r, bf16) for r in (rows, (Z, Y, C, 2, B), rows, rows, rows)]
        + [pltpu.VMEM((B, B), t) for t in (f32, f32, bf16, bf16, f32, f32, bf16, bf16)]
        + [dma((5,)), dma((4,)), dma, dma, dma, dma, dma, dma((Z,)), dma, dma, dma, dma, dma]
        + [regular((Y,)), regular((Z,))],
        compiler_params=pltpu.CompilerParams(
            collective_id=0, has_side_effects=True, vmem_limit_bytes=32 * 1024 * 1024
        ),
    )(*[pltpu.with_memory_space_constraint(x, pltpu.HBM) for x in operands])
    grafted, new_left, new_right, new_left_root, new_right_root = pl.pallas_call(
        write_out,
        out_shape=outs,
        in_specs=[pl.BlockSpec(memory_space=pltpu.VMEM)] * 5,
        out_specs=(anywhere,) * 5,
        scratch_shapes=[dma((5,))],
        compiler_params=pltpu.CompilerParams(vmem_limit_bytes=32 * 1024 * 1024),
    )(*results)
    return (
        grafted.reshape(Y * Z * C, 2, B), new_left[None], new_right[None], new_left_root[None], new_right_root[None]
    )


def solution(mesh):
    rows, blocks = P(None, "fsdp", None), P("fsdp", None, None)
    return jax.shard_map(
        shards,
        mesh=mesh,
        in_specs=(rows, P("fsdp", None), blocks, blocks, blocks, blocks),
        out_specs=(rows, blocks, blocks, blocks, blocks),
        check_vma=False,
    )
```

```python
import functools

import jax
import jax.numpy as jnp
from jax import lax
from jax.experimental import pallas as pl
from jax.experimental.pallas import tpu as pltpu
from jax.sharding import PartitionSpec as P

ITERS = 5
B = 256
Y, Z, C = 8, 8, 2

decay_rate = 0.8
epsilon = 1e-06

f32, bf16 = jnp.float32, jnp.bfloat16
MESH = pl.DeviceIdType.MESH


def dot(a, b, dims=((1,), (0,))):
    return lax.dot_general(a, b, (dims, ((), ())), preferred_element_type=f32)


def split(a, wide):
    high = a.astype(bf16)
    return (high, (a - high.astype(f32)).astype(bf16)) if wide else (high,)


def product(a, b):
    high = dot(a[0], b[0])
    return high if len(a) == 1 else high + (dot(a[0], b[1]) + dot(a[1], b[0]))


def inverse_fourth_roots(stats):
    n = range(len(stats))
    rows = lax.broadcasted_iota(jnp.int32, (B, B), 0)
    on_diagonal = rows == lax.broadcasted_iota(jnp.int32, (B, B), 1)
    frobenius = [jnp.sqrt(jnp.sum(s * s, keepdims=True)) for s in stats]
    m = [stats[i] * (0.25 / frobenius[i]) for i in n]
    root = None
    for sweep in range(ITERS):
        wide = sweep >= ITERS - 2
        parts = [split(x, wide) for x in m]
        if sweep < ITERS - 1:
            r = [dot(parts[i][0], parts[i][0]) - 2.5 * m[i] for i in n]
        if root is None:
            root = [jnp.where(on_diagonal, 1.25, 0.0) - x for x in m]
        else:
            root = [1.25 * root[i] - product(split(root[i], wide), parts[i]) for i in n]
        if sweep < ITERS - 1:
            high = [x.astype(bf16) for x in r]
            r4 = [3.125 * r[i] + dot(high[i], high[i]) for i in n]
            m = [2.44140625 * m[i] + product(split(r4[i], wide), parts[i]) for i in n]
    scale = [jnp.exp(-0.25 * jnp.log(c)) for c in frobenius]
    return [root[i] * scale[i] for i in n]


def kernel(
    refresh_ref, g_ref, ls_ref, rs_ref, lr_ref, rr_ref,
    out_ref, nl_ref, nr_ref, nlr_ref, nrr_ref,
    refresh, both, relay, block, back, both_back, ls, rs, lr, rr, nl, nr, nlr, nrr,
    load_sem, store_sem, send_core, recv_core, send_row, send_down, send_up, recv_relay, recv_block,
    send_back, recv_back, send_out, recv_out, here_row, here_up, here_corner,
):
    me, own = lax.axis_index("fsdp"), lax.axis_index("own")
    y, z, c = me // (Z * C), (me // C) % Z, me % C
    ORDER = (0, 1, 2, 3, 6, 7, 4, 5)
    rank = (jnp.where(y < 4, y, (y + 2) % 4 + 4) + jnp.where(z == 0, Y - 1, 0)) % Y
    plane = (own == 0) & (c == 0)
    corner = plane & (y == 0) & (z == 0)
    between = plane & (z > 0) & (z < Z - 1)

    def ordered(r):
        return jnp.where(z == 0, ORDER[(r + 1) % Y], ORDER[r])

    def at(py, pz, pc=c):
        return ((py * Z + pz) * C + pc, own)

    def signal(sem, device):
        pl.semaphore_signal(sem, inc=1, device_id=device, device_id_type=MESH)

    def remote(src, dst, send, recv, to):
        pltpu.make_async_remote_copy(
            src_ref=src, dst_ref=dst, send_sem=send, recv_sem=recv, device_id=to, device_id_type=MESH
        ).start()

    def local(src, dst, sem):
        pltpu.make_async_copy(src, dst, sem).start()

    def drained(ref, sem):
        pltpu.make_async_copy(ref, ref, sem).wait()

    def repeat(low, high, body):
        def step(i, carry):
            body(i)
            return carry

        lax.fori_loop(low, high, step, 0)

    barrier = pltpu.get_barrier_semaphore()
    signal(barrier, at(y, z, 1 - c))
    for r in range(1, Y):

        @pl.when(r > rank)
        def _():
            signal(barrier, at(ordered(r), z))

    @functools.partial(repeat, jnp.where(corner, Z - 1, z + 1), Z)
    def _(pz):
        for py in range(Y):
            signal(barrier, at(py, pz))

    @pl.when(between)
    def _():
        signal(barrier, at(0, 0))

    loads = [
        pltpu.make_async_copy(src, dst, load_sem.at[i])
        for i, (src, dst) in enumerate(
            ((refresh_ref, refresh), (ls_ref, ls), (rs_ref, rs), (lr_ref, lr), (rr_ref, rr))
        )
    ]
    for copy in loads:
        copy.start()
    greetings = 1 + rank + Y * z - between.astype(jnp.int32)
    pl.semaphore_wait(barrier, jnp.where(corner, 1 + rank + Y * (Z - 2), greetings))
    for r in range(Y - 1):

        @pl.when(r < rank)
        def _():
            signal(here_row.at[rank], at(ordered(r), z))

    @functools.partial(repeat, (between & (y == 0)).astype(jnp.int32), z)
    def _(pz):
        signal(here_up.at[z], at(y, pz))

    @pl.when(corner)
    def _():
        @functools.partial(repeat, 1, Z - 1)
        def _(pz):
            for py in range(Y):
                signal(here_corner, at(py, pz))

    remote(g_ref.at[:, :, 1 - c], both.at[:, :, c], send_core, recv_core, at(y, z, 1 - c))
    local(g_ref.at[:, :, c], both.at[:, :, c], recv_core)
    drained(both, recv_core)

    def to_row(py):
        remote(both.at[py, z], block.at[y, z], send_row, recv_block, at(py, z))

        @functools.partial(repeat, z + 1, Z)
        def _(pz):
            remote(both.at[py, pz], relay.at[pz, y], send_row, recv_relay.at[pz], at(py, z))

    for r in range(Y - 1):

        @pl.when(r < rank)
        def _():
            to_row(ordered(r))

    def down(py, pz):
        remote(both.at[py, pz], block.at[y, z], send_down, recv_block, at(py, pz))

    for pz in (3, 4, 0, 5, 2, 1, 6):

        @pl.when(pz < z)
        def _():
            for py in range(Y):
                if py or pz:
                    down(py, pz)
                else:
                    pl.when(jnp.logical_not(between))(functools.partial(down, 0, 0))

    local(both.at[y, z], block.at[y, z], recv_block)

    @functools.partial(repeat, z + 1, Z)
    def _(pz):
        local(both.at[y, pz], relay.at[pz, y], recv_relay.at[pz])

    for r in range(1, Y):

        @pl.when(r > rank)
        def _():
            pl.semaphore_wait(here_row.at[r], 1)
            to_row(ordered(r))

    @pl.when(between)
    def _():
        pl.semaphore_wait(here_corner, 1)
        down(0, 0)

    @functools.partial(repeat, z + 1, Z)
    def _(pz):
        drained(relay.at[pz], recv_relay.at[pz])

        @pl.when(jnp.logical_not(corner) | (pz == Z - 1))
        def _():
            pl.semaphore_wait(here_up.at[pz], 1)

        remote(relay.at[pz], block.at[:, z], send_up, recv_block, at(y, pz))

    drained(both.at[:, :, 0], send_core)
    repeat(z, Z, lambda i: drained(relay.at[0, 1:], send_row))
    repeat(0, z, lambda i: drained(relay.at[0], send_down))
    repeat(z + 1, Z, lambda i: drained(relay.at[0], send_up))
    for copy in loads:
        copy.wait()
    drained(block, recv_block)

    g = block[...].reshape(B, B)
    new_left = decay_rate * ls[...] + (1.0 - decay_rate) * dot(g, g, ((1,), (1,)))
    new_right = decay_rate * rs[...] + (1.0 - decay_rate) * dot(g, g, ((0,), (0,)))
    nl[...] = new_left
    nr[...] = new_right
    stores = [
        pltpu.make_async_copy(src, dst, store_sem.at[i])
        for i, (src, dst) in enumerate(((nl, nl_ref), (nr, nr_ref), (nlr, nlr_ref), (nrr, nrr_ref)))
    ]
    stores[0].start()
    stores[1].start()
    left_fresh, right_fresh = inverse_fourth_roots([new_left, new_right])
    left = jnp.where(refresh[0, 0] == 1, left_fresh.astype(bf16), lr[...])
    right = jnp.where(refresh[0, 1] == 1, right_fresh.astype(bf16), rr[...])
    nlr[...] = left
    nrr[...] = right
    stores[2].start()
    stores[3].start()
    preconditioned = dot(dot(left, g).astype(bf16), right)
    wide = g.astype(f32)
    grad_norm = jnp.sqrt(jnp.sum(wide * wide, keepdims=True))
    norm = jnp.sqrt(jnp.sum(preconditioned * preconditioned, keepdims=True) + epsilon)
    grafted = (preconditioned * (grad_norm / norm)).astype(bf16)
    back[...] = grafted.reshape(Y, Z, C, 2, B)

    remote(back.at[:, :, 1 - c], both_back.at[:, :, c], send_back, recv_back, at(y, z, 1 - c))
    local(back.at[:, :, c], both_back.at[:, :, c], recv_back)
    drained(both_back, recv_back)

    @functools.partial(repeat, 0, Z)
    def _(pz):
        for i in (4, 3, 5, 2, 6, 1, 7):
            py = (y + i) % Y
            remote(both_back.at[py, pz], out_ref.at[y, z], send_out, recv_out, at(py, pz))

        @pl.when(pz != z)
        def _():
            remote(both_back.at[y, pz], out_ref.at[y, z], send_out, recv_out, at(y, pz))

    local(both_back.at[y, z], out_ref.at[y, z], recv_out)
    drained(both_back.at[:, :, 0], send_back)
    for copy in stores:
        copy.wait()
    drained(out_ref, recv_out)
    drained(both_back.at[1:], send_out)
    drained(both_back.at[0, 1:], send_out)


def write_out(*refs):
    n = len(refs) // 2
    copies = [pltpu.make_async_copy(refs[i], refs[n + i], refs[-1].at[i]) for i in range(n)]
    for copy in copies:
        copy.start()
    for copy in copies:
        copy.wait()


def shards(gradient, refresh, left_stat, right_stat, left_root, right_root):
    anywhere = pl.BlockSpec(memory_space=pl.ANY)
    square = lambda dtype: jax.ShapeDtypeStruct((B, B), dtype)
    rows = (Y, Z, C, 2, B)
    outs = (jax.ShapeDtypeStruct(rows, bf16), square(f32), square(f32), square(bf16), square(bf16))
    dma, regular = pltpu.SemaphoreType.DMA, pltpu.SemaphoreType.REGULAR
    operands = (
        refresh, gradient.reshape(rows), left_stat[0], right_stat[0], left_root[0], right_root[0]
    )
    results = pl.pallas_call(
        kernel,
        out_shape=outs,
        in_specs=[anywhere] * 6,
        out_specs=(anywhere,) * 5,
        scratch_shapes=[pltpu.SMEM((1, 2), jnp.int32)]
        + [pltpu.VMEM(r, bf16) for r in (rows, (Z, Y, C, 2, B), rows, rows, rows)]
        + [pltpu.VMEM((B, B), t) for t in (f32, f32, bf16, bf16, f32, f32, bf16, bf16)]
        + [dma((5,)), dma((4,)), dma, dma, dma, dma, dma, dma((Z,)), dma, dma, dma, dma, dma]
        + [regular((Y,)), regular((Z,)), regular],
        compiler_params=pltpu.CompilerParams(
            collective_id=0, has_side_effects=True, vmem_limit_bytes=32 * 1024 * 1024
        ),
    )(*[pltpu.with_memory_space_constraint(x, pltpu.HBM) for x in operands])
    grafted, new_left, new_right, new_left_root, new_right_root = pl.pallas_call(
        write_out,
        out_shape=outs,
        in_specs=[pl.BlockSpec(memory_space=pltpu.VMEM)] * 5,
        out_specs=(anywhere,) * 5,
        scratch_shapes=[dma((5,))],
        compiler_params=pltpu.CompilerParams(vmem_limit_bytes=32 * 1024 * 1024),
    )(*results)
    return (
        grafted.reshape(Y * Z * C, 2, B), new_left[None], new_right[None], new_left_root[None], new_right_root[None]
    )


def solution(mesh):
    rows, blocks = P(None, "fsdp", None), P("fsdp", None, None)
    return jax.shard_map(
        shards,
        mesh=mesh,
        in_specs=(rows, P("fsdp", None), blocks, blocks, blocks, blocks),
        out_specs=(rows, blocks, blocks, blocks, blocks),
        check_vma=False,
    )
```

```python
import functools

import jax
import jax.numpy as jnp
from jax import lax
from jax.experimental import pallas as pl
from jax.experimental.pallas import tpu as pltpu
from jax.sharding import PartitionSpec as P

ITERS = 5
B = 256
Y, Z, C = 8, 8, 2

decay_rate = 0.8
epsilon = 1e-06

f32, bf16 = jnp.float32, jnp.bfloat16
MESH = pl.DeviceIdType.MESH


def dot(a, b, dims=((1,), (0,))):
    return lax.dot_general(a, b, (dims, ((), ())), preferred_element_type=f32)


def split(a, wide):
    high = a.astype(bf16)
    return (high, (a - high.astype(f32)).astype(bf16)) if wide else (high,)


def product(a, b):
    high = dot(a[0], b[0])
    return high if len(a) == 1 else high + (dot(a[0], b[1]) + dot(a[1], b[0]))


def inverse_fourth_roots(stats):
    n = range(len(stats))
    rows = lax.broadcasted_iota(jnp.int32, (B, B), 0)
    on_diagonal = rows == lax.broadcasted_iota(jnp.int32, (B, B), 1)
    frobenius = [jnp.sqrt(jnp.sum(s * s, keepdims=True)) for s in stats]
    m = [stats[i] * (0.25 / frobenius[i]) for i in n]
    root = None
    for sweep in range(ITERS):
        wide = sweep >= ITERS - 2
        parts = [split(x, wide) for x in m]
        if sweep < ITERS - 1:
            r = [dot(parts[i][0], parts[i][0]) - 2.5 * m[i] for i in n]
        if root is None:
            root = [jnp.where(on_diagonal, 1.25, 0.0) - x for x in m]
        else:
            root = [1.25 * root[i] - product(split(root[i], wide), parts[i]) for i in n]
        if sweep < ITERS - 1:
            high = [x.astype(bf16) for x in r]
            r4 = [3.125 * r[i] + dot(high[i], high[i]) for i in n]
            m = [2.44140625 * m[i] + product(split(r4[i], wide), parts[i]) for i in n]
    scale = [jnp.exp(-0.25 * jnp.log(c)) for c in frobenius]
    return [root[i] * scale[i] for i in n]


def kernel(
    refresh_ref, g_ref, ls_ref, rs_ref, lr_ref, rr_ref,
    out_ref, nl_ref, nr_ref, nlr_ref, nrr_ref,
    refresh, both, relay, block, back, both_back, ls, rs, lr, rr, nl, nr, nlr, nrr,
    load_sem, store_sem, send_core, recv_core, send_row, send_down, send_up, recv_relay, recv_block,
    send_back, recv_back, send_out, recv_out, here_row, here_up, here_proxy, here_corner,
):
    me, own = lax.axis_index("fsdp"), lax.axis_index("own")
    y, z, c = me // (Z * C), (me // C) % Z, me % C
    ORDER = (0, 1, 2, 3, 6, 7, 4, 5)
    rank = (jnp.where(y < 4, y, (y + 2) % 4 + 4) + jnp.where(z == 0, Y - 1, 0)) % Y

    chip = (y == 0) & (z == 0)
    plane = (own == 0) & (c == 0)
    corner, sibling = plane & chip, (own == 0) & (c == 1) & chip
    proxy = (own == 1) & (c == 0) & chip
    others = plane & jnp.logical_not(chip)
    middle = others & (z > 0) & (z < Z - 1)
    last = (z == Z - 1).astype(jnp.int32)
    count = lambda flag: flag.astype(jnp.int32)

    def ordered(r):
        return jnp.where(z == 0, ORDER[(r + 1) % Y], ORDER[r])

    def at(py, pz, pc=c, px=own):
        return ((py * Z + pz) * C + pc, px)

    def signal(sem, device):
        pl.semaphore_signal(sem, inc=1, device_id=device, device_id_type=MESH)

    def remote(src, dst, send, recv, to):
        pltpu.make_async_remote_copy(
            src_ref=src, dst_ref=dst, send_sem=send, recv_sem=recv, device_id=to, device_id_type=MESH
        ).start()

    def local(src, dst, sem):
        pltpu.make_async_copy(src, dst, sem).start()

    def drained(ref, sem):
        pltpu.make_async_copy(ref, ref, sem).wait()

    def repeat(low, high, body):
        def step(i, carry):
            body(i)
            return carry

        lax.fori_loop(low, high, step, 0)

    barrier = pltpu.get_barrier_semaphore()

    @pl.when(jnp.logical_not(corner))
    def _():
        signal(barrier, at(y, z, 1 - c))
        for r in range(1, Y):

            @pl.when(r > rank)
            def _():
                signal(barrier, at(ordered(r), z))

        @functools.partial(repeat, z + 1, Z)
        def _(pz):
            for py in range(Y):
                signal(barrier, at(py, pz))

    @pl.when(others & (z > 0))
    def _():
        signal(barrier, at(0, 0))

    @pl.when((others & (z == 0)) | sibling)
    def _():
        signal(barrier, at(0, 0, 0, 1))

    @pl.when(proxy)
    def _():
        @functools.partial(repeat, 0, Z)
        def _(pz):
            signal(barrier, at(0, pz, c, 0))

    @pl.when(corner)
    def _():
        for py in range(Y):
            signal(barrier, at(py, Z - 1))

    loads = [
        pltpu.make_async_copy(src, dst, load_sem.at[i])
        for i, (src, dst) in enumerate(
            ((refresh_ref, refresh), (ls_ref, ls), (rs_ref, rs), (lr_ref, lr), (rr_ref, rr))
        )
    ]
    for copy in loads:
        copy.start()
    greetings = 1 + rank + Y * z - count(sibling) - count(middle) + count(others & (y == 0)) + Y * count(proxy)
    pl.semaphore_wait(barrier, jnp.where(corner, 2 + rank + Y * (Z - 1), greetings))

    def gather():
        for r in range(Y - 1):

            @pl.when(r < rank)
            def _():
                signal(here_row.at[rank], at(ordered(r), z))

        to_proxy = others & (y == 0)

        @pl.when(to_proxy)
        def _():
            signal(here_proxy.at[z], at(0, 0, 0, 1))

        @functools.partial(repeat, count(to_proxy), z)
        def _(pz):
            signal(here_up.at[z], at(y, pz))

        @pl.when(jnp.logical_not(sibling))
        def _():
            remote(g_ref.at[:, :, 1 - c], both.at[:, :, c], send_core, recv_core, at(y, z, 1 - c))

        @pl.when(proxy)
        def _():
            remote(g_ref.at[:, :, 1 - c], both.at[:, :, c], send_core, recv_core, at(y, z, 1 - c, 0))

        local(g_ref.at[:, :, c], both.at[:, :, c], recv_core)
        drained(both, recv_core)

        def to_row(py, px=own):
            remote(both.at[py, z], block.at[y, z], send_row, recv_block.at[last], at(py, z, c, px))

            @functools.partial(repeat, z + 1, Z)
            def _(pz):
                remote(both.at[py, pz], relay.at[pz, y], send_row, recv_relay.at[pz], at(py, z, c, px))

        for r in range(Y - 1):

            @pl.when(r < rank)
            def _():
                to_row(ordered(r))

        def down(py, pz):
            remote(both.at[py, pz], block.at[y, z], send_down, recv_block.at[last], at(py, pz))

        for pz in (3, 4, 0, 5, 2, 1, 6):

            @pl.when(pz < z)
            def _():
                for py in range(Y):
                    if py or pz:
                        down(py, pz)
                    else:
                        pl.when(jnp.logical_not(middle))(functools.partial(down, 0, 0))

        local(both.at[y, z], block.at[y, z], recv_block.at[last])

        @functools.partial(repeat, z + 1, Z)
        def _(pz):
            local(both.at[y, pz], relay.at[pz, y], recv_relay.at[pz])

        for r in range(1, Y):
            awaited = r > rank
            if r == Y - 1:
                awaited &= jnp.logical_not(others & (z == 0))

            @pl.when(awaited)
            def _():
                pl.semaphore_wait(here_row.at[r], 1)
                to_row(ordered(r))

        @pl.when(proxy)
        def _():
            for py in range(1, Y):
                to_row(py, 0)

        @functools.partial(repeat, z + 1, Z)
        def _(pz):
            drained(relay.at[pz], recv_relay.at[pz])
            pl.semaphore_wait(here_up.at[pz], 1)
            remote(relay.at[pz], block.at[:, z], send_up, recv_block.at[0], at(y, pz))

            @pl.when(proxy)
            def _():
                pl.semaphore_wait(here_proxy.at[pz], 1)
                remote(relay.at[pz], block.at[:, z], send_up, recv_block.at[0], at(y, pz, c, 0))

        repeat(0, 1 + count(proxy) - count(sibling), lambda i: drained(both.at[:, :, 0], send_core))
        partners = Y - 1 + (Y - 1) * count(proxy) - count(others & (z == 0))
        repeat(0, partners * (Z - z), lambda i: drained(relay.at[0, 0], send_row))
        repeat(0, z, lambda i: drained(relay.at[0, 1:], send_down))
        repeat(0, z - count(middle), lambda i: drained(relay.at[0, 0], send_down))
        repeat(0, (Z - 1 - z) * (1 + count(proxy)), lambda i: drained(relay.at[0], send_up))

    pl.when(jnp.logical_not(corner))(gather)

    @pl.when(corner)
    def _():
        signal(here_corner, at(0, 0, 0, 1))
        signal(here_corner, at(0, 0, 1))

        @functools.partial(repeat, 0, Z)
        def _(pz):
            for py in range(1, Y):
                signal(here_corner, at(py, pz))

            @pl.when(pz > 0)
            def _():
                signal(here_corner, at(0, pz))

    for copy in loads:
        copy.wait()
    drained(block.at[:, : Z - 1], recv_block.at[0])

    @pl.when(proxy)
    def _():
        pl.semaphore_wait(here_corner, 1)
        remote(block.at[:, : Z - 1], block.at[:, : Z - 1], send_up, recv_block.at[0], at(0, 0, 0, 0))

    drained(block.at[:, Z - 1], recv_block.at[1])

    g = block[...].reshape(B, B)
    new_left = decay_rate * ls[...] + (1.0 - decay_rate) * dot(g, g, ((1,), (1,)))
    new_right = decay_rate * rs[...] + (1.0 - decay_rate) * dot(g, g, ((0,), (0,)))
    nl[...] = new_left
    nr[...] = new_right
    stores = [
        pltpu.make_async_copy(src, dst, store_sem.at[i])
        for i, (src, dst) in enumerate(((nl, nl_ref), (nr, nr_ref), (nlr, nlr_ref), (nrr, nrr_ref)))
    ]
    stores[0].start()
    stores[1].start()
    left_fresh, right_fresh = inverse_fourth_roots([new_left, new_right])
    left = jnp.where(refresh[0, 0] == 1, left_fresh.astype(bf16), lr[...])
    right = jnp.where(refresh[0, 1] == 1, right_fresh.astype(bf16), rr[...])
    nlr[...] = left
    nrr[...] = right
    stores[2].start()
    stores[3].start()
    preconditioned = dot(dot(left, g).astype(bf16), right)
    wide = g.astype(f32)
    grad_norm = jnp.sqrt(jnp.sum(wide * wide, keepdims=True))
    norm = jnp.sqrt(jnp.sum(preconditioned * preconditioned, keepdims=True) + epsilon)
    grafted = (preconditioned * (grad_norm / norm)).astype(bf16)
    back[...] = grafted.reshape(Y, Z, C, 2, B)

    @pl.when(others | sibling)
    def _():
        pl.semaphore_wait(here_corner, 1)

    remote(back.at[:, :, 1 - c], both_back.at[:, :, c], send_back, recv_back, at(y, z, 1 - c))
    local(back.at[:, :, c], both_back.at[:, :, c], recv_back)
    drained(both_back, recv_back)

    @functools.partial(repeat, 0, Z)
    def _(pz):
        for i in (4, 3, 5, 2, 6, 1, 7):
            py = (y + i) % Y
            remote(both_back.at[py, pz], out_ref.at[y, z], send_out, recv_out, at(py, pz))

        @pl.when(pz != z)
        def _():
            remote(both_back.at[y, pz], out_ref.at[y, z], send_out, recv_out, at(y, pz))

    local(both_back.at[y, z], out_ref.at[y, z], recv_out)
    drained(both_back.at[:, :, 0], send_back)
    for copy in stores:
        copy.wait()

    @pl.when(proxy)
    def _():
        drained(block.at[:, 1:], send_up)

    drained(out_ref, recv_out)
    drained(both_back.at[1:], send_out)
    drained(both_back.at[0, 1:], send_out)


def write_out(*refs):
    n = len(refs) // 2
    copies = [pltpu.make_async_copy(refs[i], refs[n + i], refs[-1].at[i]) for i in range(n)]
    for copy in copies:
        copy.start()
    for copy in copies:
        copy.wait()


def shards(gradient, refresh, left_stat, right_stat, left_root, right_root):
    anywhere = pl.BlockSpec(memory_space=pl.ANY)
    square = lambda dtype: jax.ShapeDtypeStruct((B, B), dtype)
    rows = (Y, Z, C, 2, B)
    outs = (jax.ShapeDtypeStruct(rows, bf16), square(f32), square(f32), square(bf16), square(bf16))
    dma, regular = pltpu.SemaphoreType.DMA, pltpu.SemaphoreType.REGULAR
    operands = (
        refresh, gradient.reshape(rows), left_stat[0], right_stat[0], left_root[0], right_root[0]
    )
    results = pl.pallas_call(
        kernel,
        out_shape=outs,
        in_specs=[anywhere] * 6,
        out_specs=(anywhere,) * 5,
        scratch_shapes=[pltpu.SMEM((1, 2), jnp.int32)]
        + [pltpu.VMEM(r, bf16) for r in (rows, (Z, Y, C, 2, B), rows, rows, rows)]
        + [pltpu.VMEM((B, B), t) for t in (f32, f32, bf16, bf16, f32, f32, bf16, bf16)]
        + [dma((5,)), dma((4,)), dma, dma, dma, dma, dma, dma((Z,)), dma((2,)), dma, dma, dma, dma]
        + [regular((Y,)), regular((Z,)), regular((Z,)), regular],
        compiler_params=pltpu.CompilerParams(
            collective_id=0, has_side_effects=True, vmem_limit_bytes=32 * 1024 * 1024
        ),
    )(*[pltpu.with_memory_space_constraint(x, pltpu.HBM) for x in operands])
    grafted, new_left, new_right, new_left_root, new_right_root = pl.pallas_call(
        write_out,
        out_shape=outs,
        in_specs=[pl.BlockSpec(memory_space=pltpu.VMEM)] * 5,
        out_specs=(anywhere,) * 5,
        scratch_shapes=[dma((5,))],
        compiler_params=pltpu.CompilerParams(vmem_limit_bytes=32 * 1024 * 1024),
    )(*results)
    return (
        grafted.reshape(Y * Z * C, 2, B), new_left[None], new_right[None], new_left_root[None], new_right_root[None]
    )


def solution(mesh):
    rows, blocks = P(None, "fsdp", None), P("fsdp", None, None)
    return jax.shard_map(
        shards,
        mesh=mesh,
        in_specs=(rows, P("fsdp", None), blocks, blocks, blocks, blocks),
        out_specs=(rows, blocks, blocks, blocks, blocks),
        check_vma=False,
    )
```

```python
import functools

import jax
import jax.numpy as jnp
from jax import lax
from jax.experimental import pallas as pl
from jax.experimental.pallas import tpu as pltpu
from jax.sharding import PartitionSpec as P

ITERS = 5
B = 256
Y, Z, C = 8, 8, 2

decay_rate = 0.8
epsilon = 1e-06

f32, bf16 = jnp.float32, jnp.bfloat16
MESH = pl.DeviceIdType.MESH


def dot(a, b, dims=((1,), (0,))):
    return lax.dot_general(a, b, (dims, ((), ())), preferred_element_type=f32)


def split(a, wide):
    high = a.astype(bf16)
    return (high, (a - high.astype(f32)).astype(bf16)) if wide else (high,)


def product(a, b):
    high = dot(a[0], b[0])
    return high if len(a) == 1 else high + (dot(a[0], b[1]) + dot(a[1], b[0]))


def inverse_fourth_roots(stats):
    n = range(len(stats))
    rows = lax.broadcasted_iota(jnp.int32, (B, B), 0)
    on_diagonal = rows == lax.broadcasted_iota(jnp.int32, (B, B), 1)
    frobenius = [jnp.sqrt(jnp.sum(s * s, keepdims=True)) for s in stats]
    m = [stats[i] * (0.25 / frobenius[i]) for i in n]
    root = None
    for sweep in range(ITERS):
        wide = sweep >= ITERS - 2
        parts = [split(x, wide) for x in m]
        if sweep < ITERS - 1:
            r = [dot(parts[i][0], parts[i][0]) - 2.5 * m[i] for i in n]
        if root is None:
            root = [jnp.where(on_diagonal, 1.25, 0.0) - x for x in m]
        else:
            root = [1.25 * root[i] - product(split(root[i], wide), parts[i]) for i in n]
        if sweep < ITERS - 1:
            high = [x.astype(bf16) for x in r]
            r4 = [3.125 * r[i] + dot(high[i], high[i]) for i in n]
            m = [2.44140625 * m[i] + product(split(r4[i], wide), parts[i]) for i in n]
    scale = [jnp.exp(-0.25 * jnp.log(c)) for c in frobenius]
    return [root[i] * scale[i] for i in n]


def kernel(
    refresh_ref, g_ref, ls_ref, rs_ref, lr_ref, rr_ref,
    out_ref, nl_ref, nr_ref, nlr_ref, nrr_ref,
    refresh, both, relay, block, back, both_back, ls, rs, lr, rr, nl, nr, nlr, nrr,
    load_sem, store_sem, send_core, recv_core, send_row, send_down, send_up, recv_relay, recv_block,
    send_back, recv_back, send_out, recv_out, here_row, here_up, here_proxy, here_corner,
):
    me, own = lax.axis_index("fsdp"), lax.axis_index("own")
    y, z, c = me // (Z * C), (me // C) % Z, me % C
    ORDER = (0, 1, 2, 3, 6, 7, 4, 5)
    rank = (jnp.where(y < 4, y, (y + 2) % 4 + 4) + jnp.where(z == 0, Y - 1, 0)) % Y

    chip = (y == 0) & (z == 0)
    plane = (own == 0) & (c == 0)
    corner, sibling = plane & chip, (own == 0) & (c == 1) & chip
    proxy = (own == 1) & (c == 0) & chip
    others = plane & jnp.logical_not(chip)
    middle = others & (z > 0) & (z < Z - 1)
    last = (z == Z - 1).astype(jnp.int32)
    count = lambda flag: flag.astype(jnp.int32)

    def ordered(r):
        return jnp.where(z == 0, ORDER[(r + 1) % Y], ORDER[r])

    def at(py, pz, pc=c, px=own):
        return ((py * Z + pz) * C + pc, px)

    def signal(sem, device):
        pl.semaphore_signal(sem, inc=1, device_id=device, device_id_type=MESH)

    def remote(src, dst, send, recv, to):
        pltpu.make_async_remote_copy(
            src_ref=src, dst_ref=dst, send_sem=send, recv_sem=recv, device_id=to, device_id_type=MESH
        ).start()

    def local(src, dst, sem):
        pltpu.make_async_copy(src, dst, sem).start()

    def drained(ref, sem):
        pltpu.make_async_copy(ref, ref, sem).wait()

    def repeat(low, high, body):
        def step(i, carry):
            body(i)
            return carry

        lax.fori_loop(low, high, step, 0)

    barrier = pltpu.get_barrier_semaphore()

    @pl.when(jnp.logical_not(corner))
    def _():
        signal(barrier, at(y, z, 1 - c))
        for r in range(1, Y):

            @pl.when(r > rank)
            def _():
                signal(barrier, at(ordered(r), z))

        @functools.partial(repeat, z + 1, Z)
        def _(pz):
            for py in range(Y):
                signal(barrier, at(py, pz))

    @pl.when(others & (z > 0))
    def _():
        signal(barrier, at(0, 0))

    @pl.when((others & (z == 0)) | sibling)
    def _():
        signal(barrier, at(0, 0, 0, 1))

    @pl.when(proxy)
    def _():
        @functools.partial(repeat, 0, Z)
        def _(pz):
            signal(barrier, at(0, pz, c, 0))

    @pl.when(corner)
    def _():
        for py in range(Y):
            signal(barrier, at(py, Z - 1))

    loads = [
        pltpu.make_async_copy(src, dst, load_sem.at[i])
        for i, (src, dst) in enumerate(
            ((refresh_ref, refresh), (ls_ref, ls), (rs_ref, rs), (lr_ref, lr), (rr_ref, rr))
        )
    ]
    greetings = 1 + rank + Y * z - count(sibling) - count(middle) + count(others & (y == 0)) + Y * count(proxy)
    pl.semaphore_wait(barrier, jnp.where(corner, 2 + rank + Y * (Z - 1), greetings))

    def announce():
        @pl.when(jnp.logical_not(sibling))
        def _():
            remote(g_ref.at[:, :, 1 - c], both.at[:, :, c], send_core, recv_core, at(y, z, 1 - c))

        @pl.when(proxy)
        def _():
            remote(g_ref.at[:, :, 1 - c], both.at[:, :, c], send_core, recv_core, at(y, z, 1 - c, 0))

        local(g_ref.at[:, :, c], both.at[:, :, c], recv_core)
        for r in range(Y - 1):

            @pl.when(r < rank)
            def _():
                signal(here_row.at[rank], at(ordered(r), z))

        to_proxy = others & (y == 0)

        @pl.when(to_proxy)
        def _():
            signal(here_proxy.at[z], at(0, 0, 0, 1))

        @functools.partial(repeat, count(to_proxy), z)
        def _(pz):
            signal(here_up.at[z], at(y, pz))

    pl.when(jnp.logical_not(corner))(announce)
    for copy in loads:
        copy.start()

    def gather():
        drained(both, recv_core)

        def to_row(py, px=own):
            remote(both.at[py, z], block.at[y, z], send_row, recv_block.at[last], at(py, z, c, px))

            @functools.partial(repeat, z + 1, Z)
            def _(pz):
                remote(both.at[py, pz], relay.at[pz, y], send_row, recv_relay.at[pz], at(py, z, c, px))

        for r in range(Y - 1):

            @pl.when(r < rank)
            def _():
                to_row(ordered(r))

        def down(py, pz):
            remote(both.at[py, pz], block.at[y, z], send_down, recv_block.at[last], at(py, pz))

        def down_to(pz, wanted):
            @pl.when(wanted & (pz < z))
            def _():
                for py in range(Y):
                    if py or pz:
                        down(py, pz)
                    else:
                        pl.when(jnp.logical_not(middle))(functools.partial(down, 0, 0))

        for pz in (3, 4, 0):
            down_to(pz, z == Z - 1)

        local(both.at[y, z], block.at[y, z], recv_block.at[last])

        @functools.partial(repeat, z + 1, Z)
        def _(pz):
            local(both.at[y, pz], relay.at[pz, y], recv_relay.at[pz])

        for r in range(1, Y):
            awaited = r > rank
            if r == Y - 1:
                awaited &= jnp.logical_not(others & (z == 0))

            @pl.when(awaited)
            def _():
                pl.semaphore_wait(here_row.at[r], 1)
                to_row(ordered(r))

        for pz in (3, 4, 0):
            down_to(pz, z < Z - 1)
        for pz in (5, 2, 1, 6):
            down_to(pz, True)

        @pl.when(proxy)
        def _():
            for py in range(1, Y):
                to_row(py, 0)

        @functools.partial(repeat, z + 1, Z)
        def _(pz):
            drained(relay.at[pz], recv_relay.at[pz])
            pl.semaphore_wait(here_up.at[pz], 1)
            remote(relay.at[pz], block.at[:, z], send_up, recv_block.at[0], at(y, pz))

            @pl.when(proxy)
            def _():
                pl.semaphore_wait(here_proxy.at[pz], 1)
                remote(relay.at[pz], block.at[:, z], send_up, recv_block.at[0], at(y, pz, c, 0))

        repeat(0, 1 + count(proxy) - count(sibling), lambda i: drained(both.at[:, :, 0], send_core))
        partners = Y - 1 + (Y - 1) * count(proxy) - count(others & (z == 0))
        repeat(0, partners * (Z - z), lambda i: drained(relay.at[0, 0], send_row))
        repeat(0, z, lambda i: drained(relay.at[0, 1:], send_down))
        repeat(0, z - count(middle), lambda i: drained(relay.at[0, 0], send_down))
        repeat(0, (Z - 1 - z) * (1 + count(proxy)), lambda i: drained(relay.at[0], send_up))

    pl.when(jnp.logical_not(corner))(gather)

    @pl.when(corner)
    def _():
        signal(here_corner, at(0, 0, 0, 1))
        signal(here_corner, at(0, 0, 1))

        @functools.partial(repeat, 0, Z)
        def _(pz):
            for py in range(1, Y):
                signal(here_corner, at(py, pz))

            @pl.when(pz > 0)
            def _():
                signal(here_corner, at(0, pz))

    for copy in loads:
        copy.wait()
    drained(block.at[:, : Z - 1], recv_block.at[0])

    @pl.when(proxy)
    def _():
        pl.semaphore_wait(here_corner, 1)
        remote(block.at[:, : Z - 1], block.at[:, : Z - 1], send_up, recv_block.at[0], at(0, 0, 0, 0))

    drained(block.at[:, Z - 1], recv_block.at[1])

    g = block[...].reshape(B, B)
    new_left = decay_rate * ls[...] + (1.0 - decay_rate) * dot(g, g, ((1,), (1,)))
    new_right = decay_rate * rs[...] + (1.0 - decay_rate) * dot(g, g, ((0,), (0,)))
    nl[...] = new_left
    nr[...] = new_right
    stores = [
        pltpu.make_async_copy(src, dst, store_sem.at[i])
        for i, (src, dst) in enumerate(((nl, nl_ref), (nr, nr_ref), (nlr, nlr_ref), (nrr, nrr_ref)))
    ]
    stores[0].start()
    stores[1].start()
    left_fresh, right_fresh = inverse_fourth_roots([new_left, new_right])
    left = jnp.where(refresh[0, 0] == 1, left_fresh.astype(bf16), lr[...])
    right = jnp.where(refresh[0, 1] == 1, right_fresh.astype(bf16), rr[...])
    nlr[...] = left
    nrr[...] = right
    stores[2].start()
    stores[3].start()
    preconditioned = dot(dot(left, g).astype(bf16), right)
    wide = g.astype(f32)
    grad_norm = jnp.sqrt(jnp.sum(wide * wide, keepdims=True))
    norm = jnp.sqrt(jnp.sum(preconditioned * preconditioned, keepdims=True) + epsilon)
    grafted = (preconditioned * (grad_norm / norm)).astype(bf16)
    back[...] = grafted.reshape(Y, Z, C, 2, B)

    @pl.when(others | sibling)
    def _():
        pl.semaphore_wait(here_corner, 1)

    remote(back.at[:, :, 1 - c], both_back.at[:, :, c], send_back, recv_back, at(y, z, 1 - c))
    local(back.at[:, :, c], both_back.at[:, :, c], recv_back)
    drained(both_back, recv_back)

    @functools.partial(repeat, 0, Z)
    def _(pz):
        for py in ORDER:

            @pl.when((pz != z) | (py != y))
            def _():
                remote(both_back.at[py, pz], out_ref.at[y, z], send_out, recv_out, at(py, pz))

    local(both_back.at[y, z], out_ref.at[y, z], recv_out)
    drained(both_back.at[:, :, 0], send_back)
    for copy in stores:
        copy.wait()

    @pl.when(proxy)
    def _():
        drained(block.at[:, 1:], send_up)

    drained(out_ref, recv_out)
    drained(both_back.at[1:], send_out)
    drained(both_back.at[0, 1:], send_out)


def write_out(*refs):
    n = len(refs) // 2
    copies = [pltpu.make_async_copy(refs[i], refs[n + i], refs[-1].at[i]) for i in range(n)]
    for copy in copies:
        copy.start()
    for copy in copies:
        copy.wait()


def shards(gradient, refresh, left_stat, right_stat, left_root, right_root):
    anywhere = pl.BlockSpec(memory_space=pl.ANY)
    square = lambda dtype: jax.ShapeDtypeStruct((B, B), dtype)
    rows = (Y, Z, C, 2, B)
    outs = (jax.ShapeDtypeStruct(rows, bf16), square(f32), square(f32), square(bf16), square(bf16))
    dma, regular = pltpu.SemaphoreType.DMA, pltpu.SemaphoreType.REGULAR
    operands = (
        refresh, gradient.reshape(rows), left_stat[0], right_stat[0], left_root[0], right_root[0]
    )
    results = pl.pallas_call(
        kernel,
        out_shape=outs,
        in_specs=[anywhere] * 6,
        out_specs=(anywhere,) * 5,
        scratch_shapes=[pltpu.SMEM((1, 2), jnp.int32)]
        + [pltpu.VMEM(r, bf16) for r in (rows, (Z, Y, C, 2, B), rows, rows, rows)]
        + [pltpu.VMEM((B, B), t) for t in (f32, f32, bf16, bf16, f32, f32, bf16, bf16)]
        + [dma((5,)), dma((4,)), dma, dma, dma, dma, dma, dma((Z,)), dma((2,)), dma, dma, dma, dma]
        + [regular((Y,)), regular((Z,)), regular((Z,)), regular],
        compiler_params=pltpu.CompilerParams(
            collective_id=0, has_side_effects=True, vmem_limit_bytes=32 * 1024 * 1024
        ),
    )(*[pltpu.with_memory_space_constraint(x, pltpu.HBM) for x in operands])
    grafted, new_left, new_right, new_left_root, new_right_root = pl.pallas_call(
        write_out,
        out_shape=outs,
        in_specs=[pl.BlockSpec(memory_space=pltpu.VMEM)] * 5,
        out_specs=(anywhere,) * 5,
        scratch_shapes=[dma((5,))],
        compiler_params=pltpu.CompilerParams(vmem_limit_bytes=32 * 1024 * 1024),
    )(*results)
    return (
        grafted.reshape(Y * Z * C, 2, B), new_left[None], new_right[None], new_left_root[None], new_right_root[None]
    )


def solution(mesh):
    rows, blocks = P(None, "fsdp", None), P("fsdp", None, None)
    return jax.shard_map(
        shards,
        mesh=mesh,
        in_specs=(rows, P("fsdp", None), blocks, blocks, blocks, blocks),
        out_specs=(rows, blocks, blocks, blocks, blocks),
        check_vma=False,
    )
```

```python
import functools

import jax
import jax.numpy as jnp
from jax import lax
from jax.experimental import pallas as pl
from jax.experimental.pallas import tpu as pltpu
from jax.sharding import PartitionSpec as P

ITERS = 5
B = 256
Y, Z, C = 8, 8, 2

decay_rate = 0.8
epsilon = 1e-06

f32, bf16 = jnp.float32, jnp.bfloat16
MESH = pl.DeviceIdType.MESH


def dot(a, b, dims=((1,), (0,))):
    return lax.dot_general(a, b, (dims, ((), ())), preferred_element_type=f32)


def split(a, wide):
    high = a.astype(bf16)
    return (high, (a - high.astype(f32)).astype(bf16)) if wide else (high,)


def product(a, b):
    high = dot(a[0], b[0])
    return high if len(a) == 1 else high + (dot(a[0], b[1]) + dot(a[1], b[0]))


def inverse_fourth_roots(stats):
    n = range(len(stats))
    rows = lax.broadcasted_iota(jnp.int32, (B, B), 0)
    on_diagonal = rows == lax.broadcasted_iota(jnp.int32, (B, B), 1)
    frobenius = [jnp.sqrt(jnp.sum(s * s, keepdims=True)) for s in stats]
    m = [stats[i] * (0.25 / frobenius[i]) for i in n]
    root = None
    for sweep in range(ITERS):
        wide = sweep >= ITERS - 2
        parts = [split(x, wide) for x in m]
        if sweep < ITERS - 1:
            r = [dot(parts[i][0], parts[i][0]) - 2.5 * m[i] for i in n]
        if root is None:
            root = [jnp.where(on_diagonal, 1.25, 0.0) - x for x in m]
        else:
            root = [1.25 * root[i] - product(split(root[i], wide), parts[i]) for i in n]
        if sweep < ITERS - 1:
            high = [x.astype(bf16) for x in r]
            r4 = [3.125 * r[i] + dot(high[i], high[i]) for i in n]
            m = [2.44140625 * m[i] + product(split(r4[i], wide), parts[i]) for i in n]
    scale = [jnp.exp(-0.25 * jnp.log(c)) for c in frobenius]
    return [root[i] * scale[i] for i in n]


def kernel(
    refresh_ref, g_ref, ls_ref, rs_ref, lr_ref, rr_ref,
    out_ref, nl_ref, nr_ref, nlr_ref, nrr_ref,
    refresh, mine, both, relay, block, back, both_back, ls, rs, lr, rr, nl, nr, nlr, nrr,
    load_sem, store_sem, send_core, recv_core, send_row, send_down, send_up, recv_relay, recv_block,
    send_back, recv_back, send_out, recv_out, here_row, here_up, here_proxy, here_corner,
):
    me, own = lax.axis_index("fsdp"), lax.axis_index("own")
    y, z, c = me // (Z * C), (me // C) % Z, me % C
    ORDER = (0, 1, 2, 3, 6, 7, 4, 5)
    rank = (jnp.where(y < 4, y, (y + 2) % 4 + 4) + jnp.where(z == 0, Y - 1, 0)) % Y

    chip = (y == 0) & (z == 0)
    plane = (own == 0) & (c == 0)
    corner, sibling = plane & chip, (own == 0) & (c == 1) & chip
    proxy = (own == 1) & (c == 0) & chip
    others = plane & jnp.logical_not(chip)
    middle = others & (z > 0) & (z < Z - 1)
    last = (z == Z - 1).astype(jnp.int32)
    count = lambda flag: flag.astype(jnp.int32)

    def ordered(r):
        return jnp.where(z == 0, ORDER[(r + 1) % Y], ORDER[r])

    def at(py, pz, pc=c, px=own):
        return ((py * Z + pz) * C + pc, px)

    def signal(sem, device):
        pl.semaphore_signal(sem, inc=1, device_id=device, device_id_type=MESH)

    def remote(src, dst, send, recv, to):
        pltpu.make_async_remote_copy(
            src_ref=src, dst_ref=dst, send_sem=send, recv_sem=recv, device_id=to, device_id_type=MESH
        ).start()

    def local(src, dst, sem):
        pltpu.make_async_copy(src, dst, sem).start()

    def drained(ref, sem):
        pltpu.make_async_copy(ref, ref, sem).wait()

    def repeat(low, high, body):
        def step(i, carry):
            body(i)
            return carry

        lax.fori_loop(low, high, step, 0)

    fetch = pltpu.make_async_copy(g_ref, mine, load_sem.at[5])
    fetch.start()

    barrier = pltpu.get_barrier_semaphore()

    @pl.when(jnp.logical_not(corner))
    def _():
        signal(barrier, at(y, z, 1 - c))
        for r in range(1, Y):

            @pl.when(r > rank)
            def _():
                signal(barrier, at(ordered(r), z))

        @functools.partial(repeat, z + 1, Z)
        def _(pz):
            for py in range(Y):
                signal(barrier, at(py, pz))

    @pl.when(others & (z > 0))
    def _():
        signal(barrier, at(0, 0))

    @pl.when((others & (z == 0)) | sibling)
    def _():
        signal(barrier, at(0, 0, 0, 1))

    @pl.when(proxy)
    def _():
        @functools.partial(repeat, 0, Z)
        def _(pz):
            signal(barrier, at(0, pz, c, 0))

    @pl.when(corner)
    def _():
        for py in range(Y):
            signal(barrier, at(py, Z - 1))

    loads = [
        pltpu.make_async_copy(src, dst, load_sem.at[i])
        for i, (src, dst) in enumerate(
            ((refresh_ref, refresh), (ls_ref, ls), (rs_ref, rs), (lr_ref, lr), (rr_ref, rr))
        )
    ]
    greetings = 1 + rank + Y * z - count(sibling) - count(middle) + count(others & (y == 0)) + Y * count(proxy)
    pl.semaphore_wait(barrier, jnp.where(corner, 2 + rank + Y * (Z - 1), greetings))

    def announce():
        for r in range(Y - 1):

            @pl.when(r < rank)
            def _():
                signal(here_row.at[rank], at(ordered(r), z))

        to_proxy = others & (y == 0)

        @pl.when(to_proxy)
        def _():
            signal(here_proxy.at[z], at(0, 0, 0, 1))

        @functools.partial(repeat, count(to_proxy), z)
        def _(pz):
            signal(here_up.at[z], at(y, pz))

        fetch.wait()

        @pl.when(jnp.logical_not(sibling))
        def _():
            remote(mine.at[:, 1 - c], both.at[:, c], send_core, recv_core, at(y, z, 1 - c))

        @pl.when(proxy)
        def _():
            remote(mine.at[:, 1 - c], both.at[:, c], send_core, recv_core, at(y, z, 1 - c, 0))

        local(mine.at[:, c], both.at[:, c], recv_core)

    pl.when(jnp.logical_not(corner))(announce)
    pl.when(corner)(fetch.wait)
    for copy in loads:
        copy.start()

    def gather():
        drained(both, recv_core)

        def to_row(py, px=own):
            remote(both.at[py * Z + z], block.at[y, z], send_row, recv_block.at[last], at(py, z, c, px))

            @functools.partial(repeat, z + 1, Z)
            def _(pz):
                remote(both.at[py * Z + pz], relay.at[pz, y], send_row, recv_relay.at[pz], at(py, z, c, px))

        for r in range(Y - 1):

            @pl.when(r < rank)
            def _():
                to_row(ordered(r))

        def down(py, pz):
            remote(both.at[py * Z + pz], block.at[y, z], send_down, recv_block.at[last], at(py, pz))

        def down_to(pz, wanted):
            @pl.when(wanted & (pz < z))
            def _():
                for py in range(Y):
                    if py or pz:
                        down(py, pz)
                    else:
                        pl.when(jnp.logical_not(middle))(functools.partial(down, 0, 0))

        for pz in (3, 4, 0):
            down_to(pz, z == Z - 1)

        local(both.at[y * Z + z], block.at[y, z], recv_block.at[last])

        @functools.partial(repeat, z + 1, Z)
        def _(pz):
            local(both.at[y * Z + pz], relay.at[pz, y], recv_relay.at[pz])

        for r in range(1, Y):
            awaited = r > rank
            if r == Y - 1:
                awaited &= jnp.logical_not(others & (z == 0))

            @pl.when(awaited)
            def _():
                pl.semaphore_wait(here_row.at[r], 1)
                to_row(ordered(r))

        for pz in (3, 4, 0):
            down_to(pz, z < Z - 1)
        for pz in (5, 2, 1, 6):
            down_to(pz, True)

        @pl.when(proxy)
        def _():
            for py in range(1, Y):
                to_row(py, 0)

        @functools.partial(repeat, z + 1, Z)
        def _(pz):
            drained(relay.at[pz], recv_relay.at[pz])
            pl.semaphore_wait(here_up.at[pz], 1)
            remote(relay.at[pz], block.at[:, z], send_up, recv_block.at[0], at(y, pz))

            @pl.when(proxy)
            def _():
                pl.semaphore_wait(here_proxy.at[pz], 1)
                remote(relay.at[pz], block.at[:, z], send_up, recv_block.at[0], at(y, pz, c, 0))

        repeat(0, 1 + count(proxy) - count(sibling), lambda i: drained(both.at[:, 0], send_core))
        partners = Y - 1 + (Y - 1) * count(proxy) - count(others & (z == 0))
        repeat(0, partners * (Z - z), lambda i: drained(relay.at[0, 0], send_row))
        repeat(0, z, lambda i: drained(relay.at[0, 1:], send_down))
        repeat(0, z - count(middle), lambda i: drained(relay.at[0, 0], send_down))
        repeat(0, (Z - 1 - z) * (1 + count(proxy)), lambda i: drained(relay.at[0], send_up))

    pl.when(jnp.logical_not(corner))(gather)

    @pl.when(corner)
    def _():
        signal(here_corner, at(0, 0, 0, 1))
        signal(here_corner, at(0, 0, 1))

        @functools.partial(repeat, 0, Z)
        def _(pz):
            for py in range(1, Y):
                signal(here_corner, at(py, pz))

            @pl.when(pz > 0)
            def _():
                signal(here_corner, at(0, pz))

    for copy in loads:
        copy.wait()
    drained(block.at[:, : Z - 1], recv_block.at[0])

    @pl.when(proxy)
    def _():
        pl.semaphore_wait(here_corner, 1)
        remote(block.at[:, : Z - 1], block.at[:, : Z - 1], send_up, recv_block.at[0], at(0, 0, 0, 0))

    drained(block.at[:, Z - 1], recv_block.at[1])

    g = block[...].reshape(B, B)
    new_left = decay_rate * ls[...] + (1.0 - decay_rate) * dot(g, g, ((1,), (1,)))
    new_right = decay_rate * rs[...] + (1.0 - decay_rate) * dot(g, g, ((0,), (0,)))
    nl[...] = new_left
    nr[...] = new_right
    stores = [
        pltpu.make_async_copy(src, dst, store_sem.at[i])
        for i, (src, dst) in enumerate(((nl, nl_ref), (nr, nr_ref), (nlr, nlr_ref), (nrr, nrr_ref)))
    ]
    stores[0].start()
    stores[1].start()
    left_fresh, right_fresh = inverse_fourth_roots([new_left, new_right])
    left = jnp.where(refresh[0, 0] == 1, left_fresh.astype(bf16), lr[...])
    right = jnp.where(refresh[0, 1] == 1, right_fresh.astype(bf16), rr[...])
    nlr[...] = left
    nrr[...] = right
    stores[2].start()
    stores[3].start()
    preconditioned = dot(dot(left, g).astype(bf16), right)
    wide = g.astype(f32)
    grad_norm = jnp.sqrt(jnp.sum(wide * wide, keepdims=True))
    norm = jnp.sqrt(jnp.sum(preconditioned * preconditioned, keepdims=True) + epsilon)
    grafted = (preconditioned * (grad_norm / norm)).astype(bf16)
    back[...] = grafted.reshape(Y * Z, C, 2, B)

    @pl.when(others | sibling)
    def _():
        pl.semaphore_wait(here_corner, 1)

    remote(back.at[:, 1 - c], both_back.at[:, c], send_back, recv_back, at(y, z, 1 - c))
    local(back.at[:, c], both_back.at[:, c], recv_back)
    drained(both_back, recv_back)

    @functools.partial(repeat, 0, Z)
    def _(pz):
        for py in ORDER:

            @pl.when((pz != z) | (py != y))
            def _():
                remote(both_back.at[py * Z + pz], out_ref.at[y, z], send_out, recv_out, at(py, pz))

    local(both_back.at[y * Z + z], out_ref.at[y, z], recv_out)
    drained(both_back.at[:, 0], send_back)
    for copy in stores:
        copy.wait()

    @pl.when(proxy)
    def _():
        drained(block.at[:, 1:], send_up)

    drained(out_ref, recv_out)
    drained(both_back.at[1:], send_out)


def write_out(*refs):
    n = len(refs) // 2
    copies = [pltpu.make_async_copy(refs[i], refs[n + i], refs[-1].at[i]) for i in range(n)]
    for copy in copies:
        copy.start()
    for copy in copies:
        copy.wait()


def shards(gradient, refresh, left_stat, right_stat, left_root, right_root):
    anywhere = pl.BlockSpec(memory_space=pl.ANY)
    square = lambda dtype: jax.ShapeDtypeStruct((B, B), dtype)
    rows, flat = (Y, Z, C, 2, B), (Y * Z, C, 2, B)
    outs = (jax.ShapeDtypeStruct(rows, bf16), square(f32), square(f32), square(bf16), square(bf16))
    dma, regular = pltpu.SemaphoreType.DMA, pltpu.SemaphoreType.REGULAR
    operands = (
        refresh, gradient.reshape(flat), left_stat[0], right_stat[0], left_root[0], right_root[0]
    )
    results = pl.pallas_call(
        kernel,
        out_shape=outs,
        in_specs=[anywhere] * 6,
        out_specs=(anywhere,) * 5,
        scratch_shapes=[pltpu.SMEM((1, 2), jnp.int32)]
        + [pltpu.VMEM(r, bf16) for r in (flat, flat, (Z, Y, C, 2, B), rows, flat, flat)]
        + [pltpu.VMEM((B, B), t) for t in (f32, f32, bf16, bf16, f32, f32, bf16, bf16)]
        + [dma((6,)), dma((4,)), dma, dma, dma, dma, dma, dma((Z,)), dma((2,)), dma, dma, dma, dma]
        + [regular((Y,)), regular((Z,)), regular((Z,)), regular],
        compiler_params=pltpu.CompilerParams(
            collective_id=0, has_side_effects=True, vmem_limit_bytes=32 * 1024 * 1024
        ),
    )(*[pltpu.with_memory_space_constraint(x, pltpu.HBM) for x in operands])
    grafted, new_left, new_right, new_left_root, new_right_root = pl.pallas_call(
        write_out,
        out_shape=outs,
        in_specs=[pl.BlockSpec(memory_space=pltpu.VMEM)] * 5,
        out_specs=(anywhere,) * 5,
        scratch_shapes=[dma((5,))],
        compiler_params=pltpu.CompilerParams(vmem_limit_bytes=32 * 1024 * 1024),
    )(*results)
    return (
        grafted.reshape(Y * Z * C, 2, B), new_left[None], new_right[None], new_left_root[None], new_right_root[None]
    )


def solution(mesh):
    rows, blocks = P(None, "fsdp", None), P("fsdp", None, None)
    return jax.shard_map(
        shards,
        mesh=mesh,
        in_specs=(rows, P("fsdp", None), blocks, blocks, blocks, blocks),
        out_specs=(rows, blocks, blocks, blocks, blocks),
        check_vma=False,
    )
```

```python
import functools

import jax
import jax.numpy as jnp
from jax import lax
from jax.experimental import pallas as pl
from jax.experimental.pallas import tpu as pltpu
from jax.sharding import PartitionSpec as P

ITERS = 5
B = 256
Y, Z, C = 8, 8, 2

decay_rate = 0.8
epsilon = 1e-06

f32, bf16 = jnp.float32, jnp.bfloat16
MESH = pl.DeviceIdType.MESH


def dot(a, b, dims=((1,), (0,))):
    return lax.dot_general(a, b, (dims, ((), ())), preferred_element_type=f32)


def split(a, wide):
    high = a.astype(bf16)
    return (high, (a - high.astype(f32)).astype(bf16)) if wide else (high,)


def product(a, b):
    high = dot(a[0], b[0])
    return high if len(a) == 1 else high + (dot(a[0], b[1]) + dot(a[1], b[0]))


def inverse_fourth_roots(stats):
    n = range(len(stats))
    rows = lax.broadcasted_iota(jnp.int32, (B, B), 0)
    on_diagonal = rows == lax.broadcasted_iota(jnp.int32, (B, B), 1)
    frobenius = [jnp.sqrt(jnp.sum(s * s, keepdims=True)) for s in stats]
    m = [stats[i] * (0.25 / frobenius[i]) for i in n]
    root = None
    for sweep in range(ITERS):
        wide = sweep >= ITERS - 2
        parts = [split(x, wide) for x in m]
        if sweep < ITERS - 1:
            r = [dot(parts[i][0], parts[i][0]) - 2.5 * m[i] for i in n]
        if root is None:
            root = [jnp.where(on_diagonal, 1.25, 0.0) - x for x in m]
        else:
            root = [1.25 * root[i] - product(split(root[i], wide), parts[i]) for i in n]
        if sweep < ITERS - 1:
            high = [x.astype(bf16) for x in r]
            r4 = [3.125 * r[i] + dot(high[i], high[i]) for i in n]
            m = [2.44140625 * m[i] + product(split(r4[i], wide), parts[i]) for i in n]
    scale = [jnp.exp(-0.25 * jnp.log(c)) for c in frobenius]
    return [root[i] * scale[i] for i in n]


def kernel(
    refresh_ref, g_ref, ls_ref, rs_ref, lr_ref, rr_ref,
    out_ref, nl_ref, nr_ref, nlr_ref, nrr_ref,
    refresh, mine, both, relay, block, back, both_back, ls, rs, lr, rr, nl, nr, nlr, nrr,
    load_sem, store_sem, send_core, recv_core, send_row, send_down, send_up, recv_relay, recv_block,
    send_back, recv_back, send_out, recv_out, here_row, here_up, here_proxy, here_corner,
):
    me, own = lax.axis_index("fsdp"), lax.axis_index("own")
    y, z, c = me // (Z * C), (me // C) % Z, me % C
    shift = jnp.where(z == 0, 1, 0)
    rank = (jnp.where(y < 4, y, 11 - y) + Y - shift) % Y

    chip = (y == 0) & (z == 0)
    plane = (own == 0) & (c == 0)
    corner, sibling = plane & chip, (own == 0) & (c == 1) & chip
    proxy = (own == 1) & (c == 0) & chip
    others = plane & jnp.logical_not(chip)
    middle = others & (z > 0) & (z < Z - 1)
    last = (z == Z - 1).astype(jnp.int32)
    count = lambda flag: flag.astype(jnp.int32)

    def ordered(r):
        place = (r + shift) & (Y - 1)
        return jnp.where(place < 4, place, 11 - place)

    def at(py, pz, pc=c, px=own):
        return ((py * Z + pz) * C + pc, px)

    def signal(sem, device):
        pl.semaphore_signal(sem, inc=1, device_id=device, device_id_type=MESH)

    def remote(src, dst, send, recv, to):
        pltpu.make_async_remote_copy(
            src_ref=src, dst_ref=dst, send_sem=send, recv_sem=recv, device_id=to, device_id_type=MESH
        ).start()

    def local(src, dst, sem):
        pltpu.make_async_copy(src, dst, sem).start()

    def drained(ref, sem):
        pltpu.make_async_copy(ref, ref, sem).wait()

    def repeat(low, high, body):
        def step(i, carry):
            body(i)
            return carry

        lax.fori_loop(low, high, step, 0)

    fetch = pltpu.make_async_copy(g_ref, mine, load_sem.at[5])
    fetch.start()

    barrier = pltpu.get_barrier_semaphore()

    @pl.when(jnp.logical_not(corner))
    def _():
        signal(barrier, at(y, z, 1 - c))
        repeat(rank + 1, Y, lambda r: signal(barrier, at(ordered(r), z)))

        @functools.partial(repeat, z + 1, Z)
        def _(pz):
            for py in range(Y):
                signal(barrier, at(py, pz))

    @pl.when(others & (z > 0))
    def _():
        signal(barrier, at(0, 0))

    @pl.when((others & (z == 0)) | sibling)
    def _():
        signal(barrier, at(0, 0, 0, 1))

    @pl.when(proxy)
    def _():
        @functools.partial(repeat, 0, Z)
        def _(pz):
            signal(barrier, at(0, pz, c, 0))

    @pl.when(corner)
    def _():
        for py in range(Y):
            signal(barrier, at(py, Z - 1))

    loads = [
        pltpu.make_async_copy(src, dst, load_sem.at[i])
        for i, (src, dst) in enumerate(
            ((refresh_ref, refresh), (ls_ref, ls), (rs_ref, rs), (lr_ref, lr), (rr_ref, rr))
        )
    ]
    greetings = 1 + rank + Y * z - count(sibling) - count(middle) + count(others & (y == 0)) + Y * count(proxy)
    pl.semaphore_wait(barrier, jnp.where(corner, 2 + rank + Y * (Z - 1), greetings))

    def announce():
        fetch.wait()

        @pl.when(jnp.logical_not(sibling))
        def _():
            remote(mine.at[:, 1 - c], both.at[:, c], send_core, recv_core, at(y, z, 1 - c))

        @pl.when(proxy)
        def _():
            remote(mine.at[:, 1 - c], both.at[:, c], send_core, recv_core, at(y, z, 1 - c, 0))

        local(mine.at[:, c], both.at[:, c], recv_core)

        repeat(0, rank, lambda r: signal(here_row.at[rank], at(ordered(r), z)))

        to_proxy = others & (y == 0)

        @pl.when(to_proxy)
        def _():
            signal(here_proxy.at[z], at(0, 0, 0, 1))

        @functools.partial(repeat, count(to_proxy), z)
        def _(pz):
            signal(here_up.at[z], at(y, pz))

    pl.when(jnp.logical_not(corner))(announce)
    pl.when(corner)(fetch.wait)
    for copy in loads:
        copy.start()

    def gather():
        drained(both, recv_core)

        def to_row(py, px=own):
            remote(both.at[py * Z + z], block.at[y, z], send_row, recv_block.at[last], at(py, z, c, px))

            @functools.partial(repeat, z + 1, Z)
            def _(pz):
                remote(both.at[py * Z + pz], relay.at[pz, y], send_row, recv_relay.at[pz], at(py, z, c, px))

        repeat(0, rank, lambda r: to_row(ordered(r)))

        def down_to(pz):
            def down(py):
                remote(both.at[py * Z + pz], block.at[y, z], send_down, recv_block.at[last], at(py, pz))

            repeat(count(middle & (pz == 0)), Y, down)

        @pl.when(z == Z - 1)
        def _():
            for pz in (3, 4, 0):
                down_to(pz)

        local(both.at[y * Z + z], block.at[y, z], recv_block.at[last])

        @functools.partial(repeat, z + 1, Z)
        def _(pz):
            local(both.at[y * Z + pz], relay.at[pz, y], recv_relay.at[pz])

        @functools.partial(repeat, rank + 1, Y - count(others & (z == 0)))
        def _(r):
            pl.semaphore_wait(here_row.at[r], 1)
            to_row(ordered(r))

        @pl.when(z == Z - 1)
        def _():
            for pz in (5, 2, 1, 6):
                down_to(pz)

        @pl.when(z < Z - 1)
        def _():
            repeat(0, z, down_to)

        @pl.when(proxy)
        def _():
            repeat(1, Y, lambda py: to_row(py, 0))

        @functools.partial(repeat, z + 1, Z)
        def _(pz):
            drained(relay.at[pz], recv_relay.at[pz])
            pl.semaphore_wait(here_up.at[pz], 1)
            remote(relay.at[pz], block.at[:, z], send_up, recv_block.at[0], at(y, pz))

            @pl.when(proxy)
            def _():
                pl.semaphore_wait(here_proxy.at[pz], 1)
                remote(relay.at[pz], block.at[:, z], send_up, recv_block.at[0], at(y, pz, c, 0))

        repeat(0, 1 + count(proxy) - count(sibling), lambda i: drained(both.at[:, 0], send_core))
        partners = Y - 1 + (Y - 1) * count(proxy) - count(others & (z == 0))
        repeat(0, partners * (Z - z), lambda i: drained(relay.at[0, 0], send_row))
        repeat(0, z, lambda i: drained(relay.at[0, 1:], send_down))
        repeat(0, z - count(middle), lambda i: drained(relay.at[0, 0], send_down))
        repeat(0, (Z - 1 - z) * (1 + count(proxy)), lambda i: drained(relay.at[0], send_up))

    pl.when(jnp.logical_not(corner))(gather)

    @pl.when(corner)
    def _():
        signal(here_corner, at(0, 0, 0, 1))
        signal(here_corner, at(0, 0, 1))

        @functools.partial(repeat, 0, Z)
        def _(pz):
            for py in range(1, Y):
                signal(here_corner, at(py, pz))

            @pl.when(pz > 0)
            def _():
                signal(here_corner, at(0, pz))

    for copy in loads:
        copy.wait()
    drained(block.at[:, : Z - 1], recv_block.at[0])

    @pl.when(proxy)
    def _():
        pl.semaphore_wait(here_corner, 1)
        remote(block.at[:, : Z - 1], block.at[:, : Z - 1], send_up, recv_block.at[0], at(0, 0, 0, 0))

    drained(block.at[:, Z - 1], recv_block.at[1])

    g = block[...].reshape(B, B)
    new_left = decay_rate * ls[...] + (1.0 - decay_rate) * dot(g, g, ((1,), (1,)))
    new_right = decay_rate * rs[...] + (1.0 - decay_rate) * dot(g, g, ((0,), (0,)))
    nl[...] = new_left
    nr[...] = new_right
    stores = [
        pltpu.make_async_copy(src, dst, store_sem.at[i])
        for i, (src, dst) in enumerate(((nl, nl_ref), (nr, nr_ref), (nlr, nlr_ref), (nrr, nrr_ref)))
    ]
    stores[0].start()
    stores[1].start()
    left_fresh, right_fresh = inverse_fourth_roots([new_left, new_right])
    left = jnp.where(refresh[0, 0] == 1, left_fresh.astype(bf16), lr[...])
    right = jnp.where(refresh[0, 1] == 1, right_fresh.astype(bf16), rr[...])
    nlr[...] = left
    nrr[...] = right
    stores[2].start()
    stores[3].start()
    preconditioned = dot(dot(left, g).astype(bf16), right)
    wide = g.astype(f32)
    grad_norm = jnp.sqrt(jnp.sum(wide * wide, keepdims=True))
    norm = jnp.sqrt(jnp.sum(preconditioned * preconditioned, keepdims=True) + epsilon)
    grafted = (preconditioned * (grad_norm / norm)).astype(bf16)
    back[...] = grafted.reshape(Y * Z, C, 2, B)

    @pl.when(others | sibling)
    def _():
        pl.semaphore_wait(here_corner, 1)

    remote(back.at[:, 1 - c], both_back.at[:, c], send_back, recv_back, at(y, z, 1 - c))
    local(back.at[:, c], both_back.at[:, c], recv_back)
    drained(both_back, recv_back)

    @functools.partial(repeat, 0, Z)
    def _(pz):
        @functools.partial(repeat, 0, Y)
        def _(py):
            @pl.when((pz != z) | (py != y))
            def _():
                remote(both_back.at[py * Z + pz], out_ref.at[y, z], send_out, recv_out, at(py, pz))

    local(both_back.at[y * Z + z], out_ref.at[y, z], recv_out)
    drained(both_back.at[:, 0], send_back)
    for copy in stores:
        copy.wait()

    @pl.when(proxy)
    def _():
        drained(block.at[:, 1:], send_up)

    drained(out_ref, recv_out)
    drained(both_back.at[1:], send_out)


def write_out(*refs):
    n = len(refs) // 2
    copies = [pltpu.make_async_copy(refs[i], refs[n + i], refs[-1].at[i]) for i in range(n)]
    for copy in copies:
        copy.start()
    for copy in copies:
        copy.wait()


def shards(gradient, refresh, left_stat, right_stat, left_root, right_root):
    anywhere = pl.BlockSpec(memory_space=pl.ANY)
    square = lambda dtype: jax.ShapeDtypeStruct((B, B), dtype)
    rows, flat = (Y, Z, C, 2, B), (Y * Z, C, 2, B)
    outs = (jax.ShapeDtypeStruct(rows, bf16), square(f32), square(f32), square(bf16), square(bf16))
    dma, regular = pltpu.SemaphoreType.DMA, pltpu.SemaphoreType.REGULAR
    operands = (
        refresh, gradient.reshape(flat), left_stat[0], right_stat[0], left_root[0], right_root[0]
    )
    results = pl.pallas_call(
        kernel,
        out_shape=outs,
        in_specs=[anywhere] * 6,
        out_specs=(anywhere,) * 5,
        scratch_shapes=[pltpu.SMEM((1, 2), jnp.int32)]
        + [pltpu.VMEM(r, bf16) for r in (flat, flat, (Z, Y, C, 2, B), rows, flat, flat)]
        + [pltpu.VMEM((B, B), t) for t in (f32, f32, bf16, bf16, f32, f32, bf16, bf16)]
        + [dma((6,)), dma((4,)), dma, dma, dma, dma, dma, dma((Z,)), dma((2,)), dma, dma, dma, dma]
        + [regular((Y,)), regular((Z,)), regular((Z,)), regular],
        compiler_params=pltpu.CompilerParams(
            collective_id=0, has_side_effects=True, vmem_limit_bytes=32 * 1024 * 1024
        ),
    )(*[pltpu.with_memory_space_constraint(x, pltpu.HBM) for x in operands])
    grafted, new_left, new_right, new_left_root, new_right_root = pl.pallas_call(
        write_out,
        out_shape=outs,
        in_specs=[pl.BlockSpec(memory_space=pltpu.VMEM)] * 5,
        out_specs=(anywhere,) * 5,
        scratch_shapes=[dma((5,))],
        compiler_params=pltpu.CompilerParams(vmem_limit_bytes=32 * 1024 * 1024),
    )(*results)
    return (
        grafted.reshape(Y * Z * C, 2, B), new_left[None], new_right[None], new_left_root[None], new_right_root[None]
    )


def solution(mesh):
    rows, blocks = P(None, "fsdp", None), P("fsdp", None, None)
    return jax.shard_map(
        shards,
        mesh=mesh,
        in_specs=(rows, P("fsdp", None), blocks, blocks, blocks, blocks),
        out_specs=(rows, blocks, blocks, blocks, blocks),
        check_vma=False,
    )
```

```python
import functools

import jax
import jax.numpy as jnp
from jax import lax
from jax.experimental import pallas as pl
from jax.experimental.pallas import tpu as pltpu
from jax.sharding import PartitionSpec as P

ITERS = 5
B = 256
Y, Z, C = 8, 8, 2

decay_rate = 0.8
epsilon = 1e-06

f32, bf16 = jnp.float32, jnp.bfloat16
MESH = pl.DeviceIdType.MESH


def dot(a, b, dims=((1,), (0,))):
    return lax.dot_general(a, b, (dims, ((), ())), preferred_element_type=f32)


def inverse_fourth_roots(stats):
    n = range(len(stats))
    rows = lax.broadcasted_iota(jnp.int32, (B, B), 0)
    on_diagonal = rows == lax.broadcasted_iota(jnp.int32, (B, B), 1)
    frobenius = [jnp.sqrt(jnp.sum(s * s, keepdims=True)) for s in stats]
    m = [stats[i] * (0.25 / frobenius[i]) for i in n]
    root = None
    for sweep in range(ITERS):
        low = [x.astype(bf16) for x in m]
        if sweep < ITERS - 1:
            r = [dot(low[i], low[i]) - 2.5 * m[i] for i in n]
        if root is None:
            root = [jnp.where(on_diagonal, 1.25, 0.0) - x for x in m]
        else:
            root = [1.25 * root[i] - dot(root[i].astype(bf16), low[i]) for i in n]
        if sweep < ITERS - 1:
            r_low = [x.astype(bf16) for x in r]
            r4 = [3.125 * r[i] + dot(r_low[i], r_low[i]) for i in n]
            m = [2.44140625 * m[i] + dot(r4[i].astype(bf16), low[i]) for i in n]
    scale = [jnp.exp(-0.25 * jnp.log(c)) for c in frobenius]
    return [root[i] * scale[i] for i in n]


def kernel(
    refresh_ref, g_ref, ls_ref, rs_ref, lr_ref, rr_ref,
    out_ref, nl_ref, nr_ref, nlr_ref, nrr_ref,
    refresh, mine, both, relay, block, back, both_back, ls, rs, lr, rr, nl, nr, nlr, nrr,
    load_sem, store_sem, send_core, recv_core, send_row, send_down, send_up, recv_relay, recv_block,
    send_back, recv_back, send_first, send_out, recv_out, here_row, here_up, here_proxy, here_corner,
):
    me, own = lax.axis_index("fsdp"), lax.axis_index("own")
    y, z, c = me // (Z * C), (me // C) % Z, me % C
    shift = jnp.where(z == 0, 1, 0)
    rank = (jnp.where(y < 4, y, 11 - y) + Y - shift) % Y

    chip = (y == 0) & (z == 0)
    plane = (own == 0) & (c == 0)
    corner, sibling = plane & chip, (own == 0) & (c == 1) & chip
    proxy = (own == 1) & (c == 0) & chip
    others = plane & jnp.logical_not(chip)
    middle = others & (z > 0) & (z < Z - 1)
    last = (z == Z - 1).astype(jnp.int32)
    count = lambda flag: flag.astype(jnp.int32)

    def ordered(r):
        place = (r + shift) & (Y - 1)
        return jnp.where(place < 4, place, 11 - place)

    def at(py, pz, pc=c, px=own):
        return ((py * Z + pz) * C + pc, px)

    def signal(sem, device):
        pl.semaphore_signal(sem, inc=1, device_id=device, device_id_type=MESH)

    def remote(src, dst, send, recv, to):
        pltpu.make_async_remote_copy(
            src_ref=src, dst_ref=dst, send_sem=send, recv_sem=recv, device_id=to, device_id_type=MESH
        ).start()

    def local(src, dst, sem):
        pltpu.make_async_copy(src, dst, sem).start()

    def drained(ref, sem):
        pltpu.make_async_copy(ref, ref, sem).wait()

    def repeat(low, high, body):
        def step(i, carry):
            body(i)
            return carry

        lax.fori_loop(low, high, step, 0)

    fetch = pltpu.make_async_copy(g_ref, mine, load_sem.at[5])
    fetch.start()

    barrier = pltpu.get_barrier_semaphore()

    @pl.when(jnp.logical_not(corner))
    def _():
        signal(barrier, at(y, z, 1 - c))
        repeat(rank + 1, Y, lambda r: signal(barrier, at(ordered(r), z)))

        @functools.partial(repeat, z + 1, Z)
        def _(pz):
            for py in range(Y):
                signal(barrier, at(py, pz))

    @pl.when(others & (z > 0))
    def _():
        signal(barrier, at(0, 0))

    @pl.when((others & (z == 0)) | sibling)
    def _():
        signal(barrier, at(0, 0, 0, 1))

    @pl.when(proxy)
    def _():
        @functools.partial(repeat, 0, Z)
        def _(pz):
            signal(barrier, at(0, pz, c, 0))

    @pl.when(corner)
    def _():
        for py in range(Y):
            signal(barrier, at(py, Z - 1))

    loads = [
        pltpu.make_async_copy(src, dst, load_sem.at[i])
        for i, (src, dst) in enumerate(
            ((refresh_ref, refresh), (ls_ref, ls), (rs_ref, rs), (lr_ref, lr), (rr_ref, rr))
        )
    ]
    greetings = 1 + rank + Y * z - count(sibling) - count(middle) + count(others & (y == 0)) + Y * count(proxy)
    pl.semaphore_wait(barrier, jnp.where(corner, 2 + rank + Y * (Z - 1), greetings))

    def announce():
        fetch.wait()

        @pl.when(jnp.logical_not(sibling))
        def _():
            remote(mine.at[:, 1 - c], both.at[:, c], send_core, recv_core, at(y, z, 1 - c))

        @pl.when(proxy)
        def _():
            remote(mine.at[:, 1 - c], both.at[:, c], send_core, recv_core, at(y, z, 1 - c, 0))

        local(mine.at[:, c], both.at[:, c], recv_core)

        repeat(0, rank, lambda r: signal(here_row.at[rank], at(ordered(r), z)))

        to_proxy = others & (y == 0)

        @pl.when(to_proxy)
        def _():
            signal(here_proxy.at[z], at(0, 0, 0, 1))

        @functools.partial(repeat, count(to_proxy), z)
        def _(pz):
            signal(here_up.at[z], at(y, pz))

    pl.when(jnp.logical_not(corner))(announce)
    pl.when(corner)(fetch.wait)
    for copy in loads:
        copy.start()

    def gather():
        drained(both, recv_core)

        def to_row(py, px=own):
            remote(both.at[py * Z + z], block.at[y, z], send_row, recv_block.at[last], at(py, z, c, px))

            @functools.partial(repeat, z + 1, Z)
            def _(pz):
                remote(both.at[py * Z + pz], relay.at[pz, y], send_row, recv_relay.at[pz], at(py, z, c, px))

        repeat(0, rank, lambda r: to_row(ordered(r)))

        def down(py, pz):
            remote(both.at[py * Z + pz], block.at[y, z], send_down, recv_block.at[last], at(py, pz))

        def down_to(pz):
            repeat(count(middle & (pz == 0)), Y, lambda py: down(py, pz))

        @pl.when(z == Z - 1)
        def _():
            for pz in (3, 4, 0):
                repeat(3, 3 + Y, lambda i, pz=pz: down(i & (Y - 1), pz))

        local(both.at[y * Z + z], block.at[y, z], recv_block.at[last])

        @functools.partial(repeat, z + 1, Z)
        def _(pz):
            local(both.at[y * Z + pz], relay.at[pz, y], recv_relay.at[pz])

        @functools.partial(repeat, rank + 1, Y - count(others & (z == 0)))
        def _(r):
            pl.semaphore_wait(here_row.at[r], 1)
            to_row(ordered(r))

        @pl.when(z == Z - 1)
        def _():
            for pz in (5, 2, 1, 6):
                repeat(3, 3 + Y, lambda i, pz=pz: down(i & (Y - 1), pz))

        @pl.when(z < Z - 1)
        def _():
            repeat(0, z, down_to)

        @pl.when(proxy)
        def _():
            repeat(1, Y, lambda py: to_row(py, 0))

        @functools.partial(repeat, z + 1, Z)
        def _(pz):
            drained(relay.at[pz], recv_relay.at[pz])
            pl.semaphore_wait(here_up.at[pz], 1)
            remote(relay.at[pz], block.at[:, z], send_up, recv_block.at[0], at(y, pz))

            @pl.when(proxy)
            def _():
                pl.semaphore_wait(here_proxy.at[pz], 1)
                remote(relay.at[pz], block.at[:, z], send_up, recv_block.at[0], at(y, pz, c, 0))

        repeat(0, 1 + count(proxy) - count(sibling), lambda i: drained(both.at[:, 0], send_core))
        partners = Y - 1 + (Y - 1) * count(proxy) - count(others & (z == 0))
        repeat(0, partners * (Z - z), lambda i: drained(relay.at[0, 0], send_row))
        repeat(0, z, lambda i: drained(relay.at[0, 1:], send_down))
        repeat(0, z - count(middle), lambda i: drained(relay.at[0, 0], send_down))
        repeat(0, (Z - 1 - z) * (1 + count(proxy)), lambda i: drained(relay.at[0], send_up))

    pl.when(jnp.logical_not(corner))(gather)

    @pl.when(corner)
    def _():
        signal(here_corner, at(0, 0, 0, 1))
        signal(here_corner, at(0, 0, 1))

        @functools.partial(repeat, 0, Z)
        def _(pz):
            for py in range(1, Y):
                signal(here_corner, at(py, pz))

            @pl.when(pz > 0)
            def _():
                signal(here_corner, at(0, pz))

    for copy in loads:
        copy.wait()
    drained(block.at[:, : Z - 1], recv_block.at[0])

    @pl.when(proxy)
    def _():
        pl.semaphore_wait(here_corner, 1)
        remote(block.at[:, : Z - 1], block.at[:, : Z - 1], send_up, recv_block.at[0], at(0, 0, 0, 0))

    drained(block.at[:, Z - 1], recv_block.at[1])

    g = block[...].reshape(B, B)
    new_left = decay_rate * ls[...] + (1.0 - decay_rate) * dot(g, g, ((1,), (1,)))
    new_right = decay_rate * rs[...] + (1.0 - decay_rate) * dot(g, g, ((0,), (0,)))
    nl[...] = new_left
    nr[...] = new_right
    stores = [
        pltpu.make_async_copy(src, dst, store_sem.at[i])
        for i, (src, dst) in enumerate(((nl, nl_ref), (nr, nr_ref), (nlr, nlr_ref), (nrr, nrr_ref)))
    ]
    stores[0].start()
    stores[1].start()
    left_fresh, right_fresh = inverse_fourth_roots([new_left, new_right])
    left = jnp.where(refresh[0, 0] == 1, left_fresh.astype(bf16), lr[...])
    right = jnp.where(refresh[0, 1] == 1, right_fresh.astype(bf16), rr[...])
    nlr[...] = left
    nrr[...] = right
    stores[2].start()
    stores[3].start()
    preconditioned = dot(dot(left, g).astype(bf16), right)
    wide = g.astype(f32)
    grad_norm = jnp.sqrt(jnp.sum(wide * wide, keepdims=True))
    norm = jnp.sqrt(jnp.sum(preconditioned * preconditioned, keepdims=True) + epsilon)
    grafted = (preconditioned * (grad_norm / norm)).astype(bf16)
    back[...] = grafted.reshape(Y * Z, C, 2, B)

    @pl.when(others | sibling)
    def _():
        pl.semaphore_wait(here_corner, 1)

    for py in range(2):
        for pc in range(C):
            here = (z == 0) & (y == py) & (c == pc)
            served = (own != 0) if py == 0 and pc == 0 else own >= 0

            @pl.when(served & jnp.logical_not(here))
            def _():
                remote(back.at[py * Z, pc], out_ref.at[y, z, c], send_first, recv_out, at(py, 0, pc))

            @pl.when(served & here)
            def _():
                local(back.at[py * Z, pc], out_ref.at[y, z, c], recv_out)

    first = (z == 0) & (y < 2) & jnp.logical_not(corner)

    remote(back.at[:, 1 - c], both_back.at[:, c], send_back, recv_back, at(y, z, 1 - c))
    local(back.at[:, c], both_back.at[:, c], recv_back)
    drained(both_back, recv_back)

    @functools.partial(repeat, 0, Z)
    def _(pz):
        @functools.partial(repeat, 0, Y)
        def _(py):
            @pl.when(((pz != z) | (py != y)) & ((pz > 0) | (py > 1) | (plane & (py == 0))))
            def _():
                remote(both_back.at[py * Z + pz], out_ref.at[y, z], send_out, recv_out, at(py, pz))

    @pl.when(jnp.logical_not(first))
    def _():
        local(both_back.at[y * Z + z], out_ref.at[y, z], recv_out)

    drained(both_back.at[:, 0], send_back)
    for copy in stores:
        copy.wait()

    @pl.when(proxy)
    def _():
        drained(block.at[:, 1:], send_up)

    drained(out_ref, recv_out)
    drained(both_back.at[4:], send_out)
    repeat(0, 1 + count(plane) + count(first), lambda i: drained(both_back.at[0], send_out))
    repeat(0, 4 - count(own == 0) - count(first), lambda i: drained(both_back.at[0, 0], send_first))


def write_out(*refs):
    n = len(refs) // 2
    copies = [pltpu.make_async_copy(refs[i], refs[n + i], refs[-1].at[i]) for i in range(n)]
    for copy in copies:
        copy.start()
    for copy in copies:
        copy.wait()


def shards(gradient, refresh, left_stat, right_stat, left_root, right_root):
    anywhere = pl.BlockSpec(memory_space=pl.ANY)
    square = lambda dtype: jax.ShapeDtypeStruct((B, B), dtype)
    rows, flat = (Y, Z, C, 2, B), (Y * Z, C, 2, B)
    outs = (jax.ShapeDtypeStruct(rows, bf16), square(f32), square(f32), square(bf16), square(bf16))
    dma, regular = pltpu.SemaphoreType.DMA, pltpu.SemaphoreType.REGULAR
    operands = (
        refresh, gradient.reshape(flat), left_stat[0], right_stat[0], left_root[0], right_root[0]
    )
    results = pl.pallas_call(
        kernel,
        out_shape=outs,
        in_specs=[anywhere] * 6,
        out_specs=(anywhere,) * 5,
        scratch_shapes=[pltpu.SMEM((1, 2), jnp.int32)]
        + [pltpu.VMEM(r, bf16) for r in (flat, flat, (Z, Y, C, 2, B), rows, flat, flat)]
        + [pltpu.VMEM((B, B), t) for t in (f32, f32, bf16, bf16, f32, f32, bf16, bf16)]
        + [dma((6,)), dma((4,)), dma, dma, dma, dma, dma, dma((Z,)), dma((2,)), dma, dma, dma, dma, dma]
        + [regular((Y,)), regular((Z,)), regular((Z,)), regular],
        compiler_params=pltpu.CompilerParams(
            collective_id=0, has_side_effects=True, vmem_limit_bytes=32 * 1024 * 1024
        ),
    )(*[pltpu.with_memory_space_constraint(x, pltpu.HBM) for x in operands])
    grafted, new_left, new_right, new_left_root, new_right_root = pl.pallas_call(
        write_out,
        out_shape=outs,
        in_specs=[pl.BlockSpec(memory_space=pltpu.VMEM)] * 5,
        out_specs=(anywhere,) * 5,
        scratch_shapes=[dma((5,))],
        compiler_params=pltpu.CompilerParams(vmem_limit_bytes=32 * 1024 * 1024),
    )(*results)
    return (
        grafted.reshape(Y * Z * C, 2, B), new_left[None], new_right[None], new_left_root[None], new_right_root[None]
    )


def solution(mesh):
    rows, blocks = P(None, "fsdp", None), P("fsdp", None, None)
    return jax.shard_map(
        shards,
        mesh=mesh,
        in_specs=(rows, P("fsdp", None), blocks, blocks, blocks, blocks),
        out_specs=(rows, blocks, blocks, blocks, blocks),
        check_vma=False,
    )
```

```python
import functools

import jax
import jax.numpy as jnp
from jax import lax
from jax.experimental import pallas as pl
from jax.experimental.pallas import tpu as pltpu
from jax.sharding import PartitionSpec as P

ITERS = 5
B = 256
Y, Z, C = 8, 8, 2

decay_rate = 0.8
epsilon = 1e-06

f32, bf16 = jnp.float32, jnp.bfloat16
MESH = pl.DeviceIdType.MESH


def dot(a, b, dims=((1,), (0,))):
    return lax.dot_general(a, b, (dims, ((), ())), preferred_element_type=f32)


def inverse_fourth_roots(stats):
    n = range(len(stats))
    rows = lax.broadcasted_iota(jnp.int32, (B, B), 0)
    on_diagonal = rows == lax.broadcasted_iota(jnp.int32, (B, B), 1)
    frobenius = [jnp.sqrt(jnp.sum(s * s, keepdims=True)) for s in stats]
    m = [stats[i] * (0.25 / frobenius[i]) for i in n]
    root = None
    for sweep in range(ITERS):
        low = [x.astype(bf16) for x in m]
        if sweep < ITERS - 1:
            r = [dot(low[i], low[i]) - 2.5 * m[i] for i in n]
        if root is None:
            root = [jnp.where(on_diagonal, 1.25, 0.0) - x for x in m]
        else:
            root = [1.25 * root[i] - dot(root[i].astype(bf16), low[i]) for i in n]
        if sweep < ITERS - 1:
            r_low = [x.astype(bf16) for x in r]
            r4 = [3.125 * r[i] + dot(r_low[i], r_low[i]) for i in n]
            m = [2.44140625 * m[i] + dot(r4[i].astype(bf16), low[i]) for i in n]
    scale = [jnp.exp(-0.25 * jnp.log(c)) for c in frobenius]
    return [root[i] * scale[i] for i in n]


def kernel(
    refresh_ref, g_ref, ls_ref, rs_ref, lr_ref, rr_ref,
    out_ref, nl_ref, nr_ref, nlr_ref, nrr_ref,
    refresh, mine, both, relay, passed, block, back, both_back, ls, rs, lr, rr, nl, nr, nlr, nrr,
    load_sem, store_sem, send_core, recv_core, send_row, send_down, send_up, recv_relay, recv_block,
    send_back, recv_back, send_first, send_out, recv_out, send_passed, recv_passed, here_row, here_up, here_proxy, here_corner,
):
    me, own = lax.axis_index("fsdp"), lax.axis_index("own")
    y, z, c = me // (Z * C), (me // C) % Z, me % C
    shift = jnp.where(z == 0, 1, 0)
    rank = (jnp.where(y < 4, y, 11 - y) + Y - shift) % Y

    chip = (y == 0) & (z == 0)
    plane = (own == 0) & (c == 0)
    corner, sibling = plane & chip, (own == 0) & (c == 1) & chip
    proxy = (own == 1) & (c == 0) & chip
    others = plane & jnp.logical_not(chip)
    middle = others & (z > 0) & (z < Z - 1)
    last = (z == Z - 1).astype(jnp.int32)
    count = lambda flag: flag.astype(jnp.int32)

    def ordered(r):
        place = (r + shift) & (Y - 1)
        return jnp.where(place < 4, place, 11 - place)

    def at(py, pz, pc=c, px=own):
        return ((py * Z + pz) * C + pc, px)

    def signal(sem, device):
        pl.semaphore_signal(sem, inc=1, device_id=device, device_id_type=MESH)

    def remote(src, dst, send, recv, to):
        pltpu.make_async_remote_copy(
            src_ref=src, dst_ref=dst, send_sem=send, recv_sem=recv, device_id=to, device_id_type=MESH
        ).start()

    def local(src, dst, sem):
        pltpu.make_async_copy(src, dst, sem).start()

    def drained(ref, sem):
        pltpu.make_async_copy(ref, ref, sem).wait()

    def repeat(low, high, body):
        def step(i, carry):
            body(i)
            return carry

        lax.fori_loop(low, high, step, 0)

    fetch = pltpu.make_async_copy(g_ref, mine, load_sem.at[5])
    fetch.start()

    barrier = pltpu.get_barrier_semaphore()

    @pl.when(jnp.logical_not(corner))
    def _():
        signal(barrier, at(y, z, 1 - c))
        repeat(rank + 1, Y, lambda r: signal(barrier, at(ordered(r), z)))

        low = jnp.where(z == Z - 2, y, 0)
        high = jnp.where(z == Z - 2, y + 1, Y)

        @functools.partial(repeat, z + 1, Z)
        def _(pz):
            repeat(low, high, lambda py: signal(barrier, at(py, pz)))

    @pl.when(others & (z > 0))
    def _():
        signal(barrier, at(0, 0))

    @pl.when((others & (z == 0)) | sibling)
    def _():
        signal(barrier, at(0, 0, 0, 1))

    @pl.when(proxy)
    def _():
        @functools.partial(repeat, 0, Z)
        def _(pz):
            signal(barrier, at(0, pz, c, 0))

    @pl.when(corner)
    def _():
        for py in range(Y):
            signal(barrier, at(py, Z - 1))

    loads = [
        pltpu.make_async_copy(src, dst, load_sem.at[i])
        for i, (src, dst) in enumerate(
            ((refresh_ref, refresh), (ls_ref, ls), (rs_ref, rs), (lr_ref, lr), (rr_ref, rr))
        )
    ]
    greetings = 1 + rank + Y * z - (Y - 1) * last - count(sibling) - count(middle) + count(others & (y == 0)) + Y * count(proxy)
    pl.semaphore_wait(barrier, jnp.where(corner, 2 + rank + Y * (Z - 1), greetings))

    def announce():
        fetch.wait()

        @pl.when(jnp.logical_not(sibling))
        def _():
            remote(mine.at[:, 1 - c], both.at[:, c], send_core, recv_core, at(y, z, 1 - c))

        @pl.when(proxy)
        def _():
            remote(mine.at[:, 1 - c], both.at[:, c], send_core, recv_core, at(y, z, 1 - c, 0))

        local(mine.at[:, c], both.at[:, c], recv_core)

        repeat(0, rank, lambda r: signal(here_row.at[rank], at(ordered(r), z)))

        to_proxy = others & (y == 0)

        @pl.when(to_proxy)
        def _():
            signal(here_proxy.at[z], at(0, 0, 0, 1))

        @functools.partial(repeat, count(to_proxy), z)
        def _(pz):
            signal(here_up.at[z], at(y, pz))

    pl.when(jnp.logical_not(corner))(announce)
    pl.when(corner)(fetch.wait)
    for copy in loads:
        copy.start()

    def gather():
        drained(both, recv_core)

        def to_row(py, px=own):
            remote(both.at[py * Z + z], block.at[y, z], send_row, recv_block.at[last], at(py, z, c, px))

            @functools.partial(repeat, z + 1, Z)
            def _(pz):
                remote(both.at[py * Z + pz], relay.at[pz, y], send_row, recv_relay.at[pz], at(py, z, c, px))

        repeat(0, rank, lambda r: to_row(ordered(r)))

        def down(py, pz):
            remote(both.at[py * Z + pz], block.at[y, z], send_down, recv_block.at[last], at(py, pz))

        def down_to(pz):
            repeat(count(middle & (pz == 0)), Y, lambda py: down(py, pz))

        @pl.when(z == Z - 1)
        def _():
            @functools.partial(repeat, y + 1, y + Y)
            def _(i):
                py = i & (Y - 1)
                remote(both.at[py * Z + Z - 2], passed.at[i - y], send_down, recv_passed, at(y, Z - 2))

            down(y, Z - 2)
            for pz in (3, 4, 0):
                repeat(3, 3 + Y, lambda i, pz=pz: down(i & (Y - 1), pz))

        local(both.at[y * Z + z], block.at[y, z], recv_block.at[last])

        @functools.partial(repeat, z + 1, Z)
        def _(pz):
            local(both.at[y * Z + pz], relay.at[pz, y], recv_relay.at[pz])

        @functools.partial(repeat, rank + 1, Y - count(others & (z == 0)))
        def _(r):
            pl.semaphore_wait(here_row.at[r], 1)
            to_row(ordered(r))

        @pl.when(z == Z - 1)
        def _():
            for pz in (5, 2, 1):
                repeat(3, 3 + Y, lambda i, pz=pz: down(i & (Y - 1), pz))

        @pl.when(z < Z - 1)
        def _():
            repeat(0, z, down_to)

        @pl.when(proxy)
        def _():
            repeat(1, Y, lambda py: to_row(py, 0))

        @functools.partial(repeat, z + 1, Z)
        def _(pz):
            drained(relay.at[pz], recv_relay.at[pz])
            pl.semaphore_wait(here_up.at[pz], 1)
            remote(relay.at[pz], block.at[:, z], send_up, recv_block.at[0], at(y, pz))

            @pl.when(proxy)
            def _():
                pl.semaphore_wait(here_proxy.at[pz], 1)
                remote(relay.at[pz], block.at[:, z], send_up, recv_block.at[0], at(y, pz, c, 0))

        @pl.when(z == Z - 2)
        def _():
            drained(passed.at[1:], recv_passed)

            @functools.partial(repeat, y + 1, y + Y)
            def _(i):
                py = i & (Y - 1)
                remote(passed.at[i - y], block.at[y, Z - 1], send_passed, recv_block.at[1], at(py, Z - 2))

            drained(passed.at[1:], send_passed)

        repeat(0, 1 + count(proxy) - count(sibling), lambda i: drained(both.at[:, 0], send_core))
        partners = Y - 1 + (Y - 1) * count(proxy) - count(others & (z == 0))
        repeat(0, partners * (Z - z), lambda i: drained(relay.at[0, 0], send_row))
        repeat(0, z, lambda i: drained(relay.at[0, 1:], send_down))
        repeat(0, z - count(middle), lambda i: drained(relay.at[0, 0], send_down))
        repeat(0, (Z - 1 - z) * (1 + count(proxy)), lambda i: drained(relay.at[0], send_up))

    pl.when(jnp.logical_not(corner))(gather)

    @pl.when(corner)
    def _():
        signal(here_corner, at(0, 0, 0, 1))
        signal(here_corner, at(0, 0, 1))

        @functools.partial(repeat, 0, Z)
        def _(pz):
            for py in range(1, Y):
                signal(here_corner, at(py, pz))

            @pl.when(pz > 0)
            def _():
                signal(here_corner, at(0, pz))

    for copy in loads:
        copy.wait()
    drained(block.at[:, : Z - 1], recv_block.at[0])

    @pl.when(proxy)
    def _():
        pl.semaphore_wait(here_corner, 1)
        remote(block.at[:, : Z - 1], block.at[:, : Z - 1], send_up, recv_block.at[0], at(0, 0, 0, 0))

    drained(block.at[:, Z - 1], recv_block.at[1])

    g = block[...].reshape(B, B)
    new_left = decay_rate * ls[...] + (1.0 - decay_rate) * dot(g, g, ((1,), (1,)))
    new_right = decay_rate * rs[...] + (1.0 - decay_rate) * dot(g, g, ((0,), (0,)))
    nl[...] = new_left
    nr[...] = new_right
    stores = [
        pltpu.make_async_copy(src, dst, store_sem.at[i])
        for i, (src, dst) in enumerate(((nl, nl_ref), (nr, nr_ref), (nlr, nlr_ref), (nrr, nrr_ref)))
    ]
    stores[0].start()
    stores[1].start()
    left_fresh, right_fresh = inverse_fourth_roots([new_left, new_right])
    left = jnp.where(refresh[0, 0] == 1, left_fresh.astype(bf16), lr[...])
    right = jnp.where(refresh[0, 1] == 1, right_fresh.astype(bf16), rr[...])
    nlr[...] = left
    nrr[...] = right
    stores[2].start()
    stores[3].start()
    preconditioned = dot(dot(left, g).astype(bf16), right)
    wide = g.astype(f32)
    grad_norm = jnp.sqrt(jnp.sum(wide * wide, keepdims=True))
    norm = jnp.sqrt(jnp.sum(preconditioned * preconditioned, keepdims=True) + epsilon)
    grafted = (preconditioned * (grad_norm / norm)).astype(bf16)
    back[...] = grafted.reshape(Y * Z, C, 2, B)

    @pl.when(others | sibling)
    def _():
        pl.semaphore_wait(here_corner, 1)

    for py in range(2):
        for pc in range(C):
            here = (z == 0) & (y == py) & (c == pc)
            served = (own != 0) if py == 0 and pc == 0 else own >= 0

            @pl.when(served & jnp.logical_not(here))
            def _():
                remote(back.at[py * Z, pc], out_ref.at[y, z, c], send_first, recv_out, at(py, 0, pc))

            @pl.when(served & here)
            def _():
                local(back.at[py * Z, pc], out_ref.at[y, z, c], recv_out)

    first = (z == 0) & (y < 2) & jnp.logical_not(corner)

    remote(back.at[:, 1 - c], both_back.at[:, c], send_back, recv_back, at(y, z, 1 - c))
    local(back.at[:, c], both_back.at[:, c], recv_back)
    drained(both_back, recv_back)

    @functools.partial(repeat, 0, Z)
    def _(pz):
        @functools.partial(repeat, 0, Y)
        def _(py):
            @pl.when(((pz != z) | (py != y)) & ((pz > 0) | (py > 1) | (plane & (py == 0))))
            def _():
                remote(both_back.at[py * Z + pz], out_ref.at[y, z], send_out, recv_out, at(py, pz))

    @pl.when(jnp.logical_not(first))
    def _():
        local(both_back.at[y * Z + z], out_ref.at[y, z], recv_out)

    drained(both_back.at[:, 0], send_back)
    for copy in stores:
        copy.wait()

    @pl.when(proxy)
    def _():
        drained(block.at[:, 1:], send_up)

    drained(out_ref, recv_out)
    drained(both_back.at[4:], send_out)
    repeat(0, 1 + count(plane) + count(first), lambda i: drained(both_back.at[0], send_out))
    repeat(0, 4 - count(own == 0) - count(first), lambda i: drained(both_back.at[0, 0], send_first))


def write_out(*refs):
    n = len(refs) // 2
    copies = [pltpu.make_async_copy(refs[i], refs[n + i], refs[-1].at[i]) for i in range(n)]
    for copy in copies:
        copy.start()
    for copy in copies:
        copy.wait()


def shards(gradient, refresh, left_stat, right_stat, left_root, right_root):
    anywhere = pl.BlockSpec(memory_space=pl.ANY)
    square = lambda dtype: jax.ShapeDtypeStruct((B, B), dtype)
    rows, flat = (Y, Z, C, 2, B), (Y * Z, C, 2, B)
    outs = (jax.ShapeDtypeStruct(rows, bf16), square(f32), square(f32), square(bf16), square(bf16))
    dma, regular = pltpu.SemaphoreType.DMA, pltpu.SemaphoreType.REGULAR
    operands = (
        refresh, gradient.reshape(flat), left_stat[0], right_stat[0], left_root[0], right_root[0]
    )
    results = pl.pallas_call(
        kernel,
        out_shape=outs,
        in_specs=[anywhere] * 6,
        out_specs=(anywhere,) * 5,
        scratch_shapes=[pltpu.SMEM((1, 2), jnp.int32)]
        + [pltpu.VMEM(r, bf16) for r in (flat, flat, (Z, Y, C, 2, B), (Y, C, 2, B), rows, flat, flat)]
        + [pltpu.VMEM((B, B), t) for t in (f32, f32, bf16, bf16, f32, f32, bf16, bf16)]
        + [dma((6,)), dma((4,)), dma, dma, dma, dma, dma, dma((Z,)), dma((2,)), dma, dma, dma, dma, dma, dma, dma]
        + [regular((Y,)), regular((Z,)), regular((Z,)), regular],
        compiler_params=pltpu.CompilerParams(
            collective_id=0, has_side_effects=True, vmem_limit_bytes=32 * 1024 * 1024
        ),
    )(*[pltpu.with_memory_space_constraint(x, pltpu.HBM) for x in operands])
    grafted, new_left, new_right, new_left_root, new_right_root = pl.pallas_call(
        write_out,
        out_shape=outs,
        in_specs=[pl.BlockSpec(memory_space=pltpu.VMEM)] * 5,
        out_specs=(anywhere,) * 5,
        scratch_shapes=[dma((5,))],
        compiler_params=pltpu.CompilerParams(vmem_limit_bytes=32 * 1024 * 1024),
    )(*results)
    return (
        grafted.reshape(Y * Z * C, 2, B), new_left[None], new_right[None], new_left_root[None], new_right_root[None]
    )


def solution(mesh):
    rows, blocks = P(None, "fsdp", None), P("fsdp", None, None)
    return jax.shard_map(
        shards,
        mesh=mesh,
        in_specs=(rows, P("fsdp", None), blocks, blocks, blocks, blocks),
        out_specs=(rows, blocks, blocks, blocks, blocks),
        check_vma=False,
    )
```

```python
import functools

import jax
import jax.numpy as jnp
from jax import lax
from jax.experimental import pallas as pl
from jax.experimental.pallas import tpu as pltpu
from jax.sharding import PartitionSpec as P

ITERS = 5
B = 256
Y, Z, C = 8, 8, 2

decay_rate = 0.8
epsilon = 1e-06

f32, bf16 = jnp.float32, jnp.bfloat16
MESH = pl.DeviceIdType.MESH


def dot(a, b, dims=((1,), (0,))):
    return lax.dot_general(a, b, (dims, ((), ())), preferred_element_type=f32)


def inverse_fourth_roots(stats):
    n = range(len(stats))
    rows = lax.broadcasted_iota(jnp.int32, (B, B), 0)
    on_diagonal = rows == lax.broadcasted_iota(jnp.int32, (B, B), 1)
    frobenius = [jnp.sqrt(jnp.sum(s * s, keepdims=True)) for s in stats]
    m = [stats[i] * (0.25 / frobenius[i]) for i in n]
    root = None
    for sweep in range(ITERS):
        low = [x.astype(bf16) for x in m]
        if sweep < ITERS - 1:
            r = [dot(low[i], low[i]) - 2.5 * m[i] for i in n]
        if root is None:
            root = [jnp.where(on_diagonal, 1.25, 0.0) - x for x in m]
        else:
            root = [1.25 * root[i] - dot(root[i].astype(bf16), low[i]) for i in n]
        if sweep < ITERS - 1:
            r_low = [x.astype(bf16) for x in r]
            r4 = [3.125 * r[i] + dot(r_low[i], r_low[i]) for i in n]
            m = [2.44140625 * m[i] + dot(r4[i].astype(bf16), low[i]) for i in n]
    scale = [jnp.exp(-0.25 * jnp.log(c)) for c in frobenius]
    return [root[i] * scale[i] for i in n]


def kernel(
    refresh_ref, g_ref, ls_ref, rs_ref, lr_ref, rr_ref,
    out_ref, nl_ref, nr_ref, nlr_ref, nrr_ref,
    refresh, mine, both, relay, passed, block, back, both_back, ls, rs, lr, rr, nl, nr, nlr, nrr,
    load_sem, store_sem, send_core, recv_core, send_row, send_down, send_up, recv_relay, recv_block,
    send_back, recv_back, send_first, send_out, recv_out, send_passed, recv_passed, here_row, here_up, here_proxy, here_corner,
):
    me, own = lax.axis_index("fsdp"), lax.axis_index("own")
    y, z, c = me // (Z * C), (me // C) % Z, me % C
    shift = jnp.where(z == 0, 1, 0)
    rank = (jnp.where(y < 4, y, 11 - y) + Y - shift) % Y

    chip = (y == 0) & (z == 0)
    plane = (own == 0) & (c == 0)
    corner, sibling = plane & chip, (own == 0) & (c == 1) & chip
    proxy = (own == 1) & (c == 0) & chip
    others = plane & jnp.logical_not(chip)
    middle = others & (z > 0) & (z < Z - 1)
    last = (z == Z - 1).astype(jnp.int32)
    count = lambda flag: flag.astype(jnp.int32)

    def ordered(r):
        place = (r + shift) & (Y - 1)
        return jnp.where(place < 4, place, 11 - place)

    def at(py, pz, pc=c, px=own):
        return ((py * Z + pz) * C + pc, px)

    def signal(sem, device):
        pl.semaphore_signal(sem, inc=1, device_id=device, device_id_type=MESH)

    def remote(src, dst, send, recv, to):
        pltpu.make_async_remote_copy(
            src_ref=src, dst_ref=dst, send_sem=send, recv_sem=recv, device_id=to, device_id_type=MESH
        ).start()

    def local(src, dst, sem):
        pltpu.make_async_copy(src, dst, sem).start()

    def drained(ref, sem):
        pltpu.make_async_copy(ref, ref, sem).wait()

    def repeat(low, high, body):
        def step(i, carry):
            body(i)
            return carry

        lax.fori_loop(low, high, step, 0)

    fetch = pltpu.make_async_copy(g_ref, mine, load_sem.at[5])
    fetch.start()

    barrier = pltpu.get_barrier_semaphore()

    @pl.when(jnp.logical_not(corner))
    def _():
        signal(barrier, at(y, z, 1 - c))
        repeat(rank + 1, Y, lambda r: signal(barrier, at(ordered(r), z)))

        low = jnp.where(z == Z - 2, y, 0)
        high = jnp.where(z == Z - 2, y + 1, Y)

        @functools.partial(repeat, z + 1, Z)
        def _(pz):
            repeat(low, high, lambda py: signal(barrier, at(py, pz)))

    @pl.when(others & (z > 0))
    def _():
        signal(barrier, at(0, 0))

    @pl.when((others & (z == 0)) | sibling)
    def _():
        signal(barrier, at(0, 0, 0, 1))

    @pl.when(proxy)
    def _():
        @functools.partial(repeat, 0, Z)
        def _(pz):
            signal(barrier, at(0, pz, c, 0))

    @pl.when(corner)
    def _():
        for py in range(Y):
            signal(barrier, at(py, Z - 1))

    loads = [
        pltpu.make_async_copy(src, dst, load_sem.at[i])
        for i, (src, dst) in enumerate(
            ((refresh_ref, refresh), (ls_ref, ls), (rs_ref, rs), (lr_ref, lr), (rr_ref, rr))
        )
    ]
    greetings = 1 + rank + Y * z - (Y - 1) * last - count(sibling) - count(middle) + count(others & (y == 0)) + Y * count(proxy)
    pl.semaphore_wait(barrier, jnp.where(corner, 2 + rank + Y * (Z - 1), greetings))

    def announce():
        fetch.wait()

        @pl.when(jnp.logical_not(sibling))
        def _():
            remote(mine.at[:, 1 - c], both.at[:, c], send_core, recv_core, at(y, z, 1 - c))

        @pl.when(proxy)
        def _():
            remote(mine.at[:, 1 - c], both.at[:, c], send_core, recv_core, at(y, z, 1 - c, 0))

        local(mine.at[:, c], both.at[:, c], recv_core)

        repeat(0, rank, lambda r: signal(here_row.at[rank], at(ordered(r), z)))

        to_proxy = others & (y == 0)

        @pl.when(to_proxy)
        def _():
            signal(here_proxy.at[z], at(0, 0, 0, 1))

        @functools.partial(repeat, count(to_proxy), z)
        def _(pz):
            signal(here_up.at[z], at(y, pz))

    pl.when(jnp.logical_not(corner))(announce)
    pl.when(corner)(fetch.wait)
    for copy in loads:
        copy.start()

    def gather():
        drained(both, recv_core)

        def to_row(py, px=own):
            remote(both.at[py * Z + z], block.at[y, z], send_row, recv_block.at[last], at(py, z, c, px))

            @functools.partial(repeat, z + 1, Z)
            def _(pz):
                remote(both.at[py * Z + pz], relay.at[pz, y], send_row, recv_relay.at[pz], at(py, z, c, px))

        repeat(0, rank, lambda r: to_row(ordered(r)))

        def down(py, pz):
            remote(both.at[py * Z + pz], block.at[y, z], send_down, recv_block.at[last], at(py, pz))

        def down_to(pz):
            repeat(count(middle & (pz == 0)), Y, lambda py: down(py, pz))

        @pl.when(z == Z - 1)
        def _():
            for pz in (3, 4, 0):
                repeat(3, 3 + Y, lambda i, pz=pz: down(i & (Y - 1), pz))

        local(both.at[y * Z + z], block.at[y, z], recv_block.at[last])

        @functools.partial(repeat, z + 1, Z)
        def _(pz):
            local(both.at[y * Z + pz], relay.at[pz, y], recv_relay.at[pz])

        @functools.partial(repeat, rank + 1, Y - count(others & (z == 0)))
        def _(r):
            pl.semaphore_wait(here_row.at[r], 1)
            to_row(ordered(r))

        @pl.when(z == Z - 1)
        def _():
            @functools.partial(repeat, y + 1, y + Y)
            def _(i):
                py = i & (Y - 1)
                remote(both.at[py * Z + Z - 2], passed.at[i - y], send_down, recv_passed, at(y, Z - 2))

            down(y, Z - 2)
            for pz in (5, 2, 1):
                repeat(3, 3 + Y, lambda i, pz=pz: down(i & (Y - 1), pz))

        @pl.when(z < Z - 1)
        def _():
            repeat(0, z, down_to)

        @pl.when(proxy)
        def _():
            repeat(1, Y, lambda py: to_row(py, 0))

        @functools.partial(repeat, z + 1, Z)
        def _(pz):
            drained(relay.at[pz], recv_relay.at[pz])
            pl.semaphore_wait(here_up.at[pz], 1)
            remote(relay.at[pz], block.at[:, z], send_up, recv_block.at[0], at(y, pz))

            @pl.when(proxy)
            def _():
                pl.semaphore_wait(here_proxy.at[pz], 1)
                remote(relay.at[pz], block.at[:, z], send_up, recv_block.at[0], at(y, pz, c, 0))

        @pl.when(z == Z - 2)
        def _():
            drained(passed.at[1:], recv_passed)

            @functools.partial(repeat, y + 1, y + Y)
            def _(i):
                py = i & (Y - 1)
                remote(passed.at[i - y], block.at[y, Z - 1], send_passed, recv_block.at[1], at(py, Z - 2))

            drained(passed.at[1:], send_passed)

        repeat(0, 1 + count(proxy) - count(sibling), lambda i: drained(both.at[:, 0], send_core))
        partners = Y - 1 + (Y - 1) * count(proxy) - count(others & (z == 0))
        repeat(0, partners * (Z - z), lambda i: drained(relay.at[0, 0], send_row))
        repeat(0, z, lambda i: drained(relay.at[0, 1:], send_down))
        repeat(0, z - count(middle), lambda i: drained(relay.at[0, 0], send_down))
        repeat(0, (Z - 1 - z) * (1 + count(proxy)), lambda i: drained(relay.at[0], send_up))

    pl.when(jnp.logical_not(corner))(gather)

    @pl.when(corner)
    def _():
        signal(here_corner, at(0, 0, 0, 1))
        signal(here_corner, at(0, 0, 1))

        @functools.partial(repeat, 0, Z)
        def _(pz):
            for py in range(1, Y):
                signal(here_corner, at(py, pz))

            @pl.when(pz > 0)
            def _():
                signal(here_corner, at(0, pz))

    for copy in loads:
        copy.wait()
    drained(block.at[:, : Z - 1], recv_block.at[0])

    @pl.when(proxy)
    def _():
        pl.semaphore_wait(here_corner, 1)
        remote(block.at[:, : Z - 1], block.at[:, : Z - 1], send_up, recv_block.at[0], at(0, 0, 0, 0))

    drained(block.at[:, Z - 1], recv_block.at[1])

    g = block[...].reshape(B, B)
    new_left = decay_rate * ls[...] + (1.0 - decay_rate) * dot(g, g, ((1,), (1,)))
    new_right = decay_rate * rs[...] + (1.0 - decay_rate) * dot(g, g, ((0,), (0,)))
    nl[...] = new_left
    nr[...] = new_right
    stores = [
        pltpu.make_async_copy(src, dst, store_sem.at[i])
        for i, (src, dst) in enumerate(((nl, nl_ref), (nr, nr_ref), (nlr, nlr_ref), (nrr, nrr_ref)))
    ]
    stores[0].start()
    stores[1].start()
    left_fresh, right_fresh = inverse_fourth_roots([new_left, new_right])
    left = jnp.where(refresh[0, 0] == 1, left_fresh.astype(bf16), lr[...])
    right = jnp.where(refresh[0, 1] == 1, right_fresh.astype(bf16), rr[...])
    nlr[...] = left
    nrr[...] = right
    stores[2].start()
    stores[3].start()
    preconditioned = dot(dot(left, g).astype(bf16), right)
    wide = g.astype(f32)
    grad_norm = jnp.sqrt(jnp.sum(wide * wide, keepdims=True))
    norm = jnp.sqrt(jnp.sum(preconditioned * preconditioned, keepdims=True) + epsilon)
    grafted = (preconditioned * (grad_norm / norm)).astype(bf16)
    back[...] = grafted.reshape(Y * Z, C, 2, B)

    @pl.when(others | sibling)
    def _():
        pl.semaphore_wait(here_corner, 1)

    for py in range(2):
        for pc in range(C):
            here = (z == 0) & (y == py) & (c == pc)
            served = (own != 0) if py == 0 and pc == 0 else own >= 0

            @pl.when(served & jnp.logical_not(here))
            def _():
                remote(back.at[py * Z, pc], out_ref.at[y, z, c], send_first, recv_out, at(py, 0, pc))

            @pl.when(served & here)
            def _():
                local(back.at[py * Z, pc], out_ref.at[y, z, c], recv_out)

    first = (z == 0) & (y < 2) & jnp.logical_not(corner)

    remote(back.at[:, 1 - c], both_back.at[:, c], send_back, recv_back, at(y, z, 1 - c))
    local(back.at[:, c], both_back.at[:, c], recv_back)
    drained(both_back, recv_back)

    @functools.partial(repeat, 0, Z)
    def _(pz):
        @functools.partial(repeat, 0, Y)
        def _(py):
            @pl.when(((pz != z) | (py != y)) & ((pz > 0) | (py > 1) | (plane & (py == 0))))
            def _():
                remote(both_back.at[py * Z + pz], out_ref.at[y, z], send_out, recv_out, at(py, pz))

    @pl.when(jnp.logical_not(first))
    def _():
        local(both_back.at[y * Z + z], out_ref.at[y, z], recv_out)

    drained(both_back.at[:, 0], send_back)
    for copy in stores:
        copy.wait()

    @pl.when(proxy)
    def _():
        drained(block.at[:, 1:], send_up)

    drained(out_ref, recv_out)
    drained(both_back.at[4:], send_out)
    repeat(0, 1 + count(plane) + count(first), lambda i: drained(both_back.at[0], send_out))
    repeat(0, 4 - count(own == 0) - count(first), lambda i: drained(both_back.at[0, 0], send_first))


def write_out(*refs):
    n = len(refs) // 2
    copies = [pltpu.make_async_copy(refs[i], refs[n + i], refs[-1].at[i]) for i in range(n)]
    for copy in copies:
        copy.start()
    for copy in copies:
        copy.wait()


def shards(gradient, refresh, left_stat, right_stat, left_root, right_root):
    anywhere = pl.BlockSpec(memory_space=pl.ANY)
    square = lambda dtype: jax.ShapeDtypeStruct((B, B), dtype)
    rows, flat = (Y, Z, C, 2, B), (Y * Z, C, 2, B)
    outs = (jax.ShapeDtypeStruct(rows, bf16), square(f32), square(f32), square(bf16), square(bf16))
    dma, regular = pltpu.SemaphoreType.DMA, pltpu.SemaphoreType.REGULAR
    operands = (
        refresh, gradient.reshape(flat), left_stat[0], right_stat[0], left_root[0], right_root[0]
    )
    results = pl.pallas_call(
        kernel,
        out_shape=outs,
        in_specs=[anywhere] * 6,
        out_specs=(anywhere,) * 5,
        scratch_shapes=[pltpu.SMEM((1, 2), jnp.int32)]
        + [pltpu.VMEM(r, bf16) for r in (flat, flat, (Z, Y, C, 2, B), (Y, C, 2, B), rows, flat, flat)]
        + [pltpu.VMEM((B, B), t) for t in (f32, f32, bf16, bf16, f32, f32, bf16, bf16)]
        + [dma((6,)), dma((4,)), dma, dma, dma, dma, dma, dma((Z,)), dma((2,)), dma, dma, dma, dma, dma, dma, dma]
        + [regular((Y,)), regular((Z,)), regular((Z,)), regular],
        compiler_params=pltpu.CompilerParams(
            collective_id=0, has_side_effects=True, vmem_limit_bytes=32 * 1024 * 1024
        ),
    )(*[pltpu.with_memory_space_constraint(x, pltpu.HBM) for x in operands])
    grafted, new_left, new_right, new_left_root, new_right_root = pl.pallas_call(
        write_out,
        out_shape=outs,
        in_specs=[pl.BlockSpec(memory_space=pltpu.VMEM)] * 5,
        out_specs=(anywhere,) * 5,
        scratch_shapes=[dma((5,))],
        compiler_params=pltpu.CompilerParams(vmem_limit_bytes=32 * 1024 * 1024),
    )(*results)
    return (
        grafted.reshape(Y * Z * C, 2, B), new_left[None], new_right[None], new_left_root[None], new_right_root[None]
    )


def solution(mesh):
    rows, blocks = P(None, "fsdp", None), P("fsdp", None, None)
    return jax.shard_map(
        shards,
        mesh=mesh,
        in_specs=(rows, P("fsdp", None), blocks, blocks, blocks, blocks),
        out_specs=(rows, blocks, blocks, blocks, blocks),
        check_vma=False,
    )
```
